32 devices in a mesh: grp: 2 (over y), seq: 16 (over z, x, core).
Axes of the slice: x: 2, y: 2, z: 4, core: 2. Of those that a mesh axis runs over, the one named last changes fastest.
Arguments:
- student_rows: bfloat16 [16384, 3584], P(('grp', 'seq')), parts along dimension 0, may hold values from -6 to 6
- teacher_rows: bfloat16 [16384, 4608], P(('grp', 'seq')), parts along dimension 0, may hold values from -6 to 6
- student_head: bfloat16 [2048, 3584], P('seq'), may hold values from -0.09375 to 0.09375
- teacher_head: bfloat16 [2048, 4608], P('seq'), may hold values from -0.09375 to 0.09375
- student_lse: bfloat16 [16384], P(('grp', 'seq')), parts along dimension 0, may hold values from 0.5 to 2.5
- teacher_lse: bfloat16 [16384], P(('grp', 'seq')), parts along dimension 0, may hold values from 0.5 to 2.5
- targets: int32 [16384], P(('grp', 'seq')), parts along dimension 0, may hold values from 0 to 2047
Outputs:
- head_grad: bfloat16 [4096, 3584], P(('grp', 'seq')), parts along dimension 0
- rows_grad: bfloat16 [16384, 3584], P(('grp', 'seq')), parts along dimension 0
- row_loss: float32 [16384], P(('grp', 'seq')), parts along dimension 0
The draws below stay inside these ranges and needn't reach their ends.
There are 2 independent parts, one for each index of `grp`. The reference program is written for one: setup_inputs(seed, part) draws one part's arguments, and reference() takes and returns one part's arrays. A program takes and returns all parts, laid end to end along the dimension named above; an argument that names none is the same for every part. Nothing has to cross between parts.
All inputs are finite; a program needn't handle non-finite values.
Results may differ from the reference program's by a relative error of at most 0.006.
Values may be sent and summed in bfloat16 or wider, within the bound.
No kernel may reach another device: no remote copies, remote signals or barrier semaphores. Data moves between devices by JAX's collectives and lax.ppermute only.
A program may use at most 64 MiB of HBM per device.

```python
import jax
import jax.numpy as jnp
from jax import lax

DS = 3584
DT = 4608
VP = 128
TOK_DEV = 512
STEPS = 4
TOKENS = 8192
VOCAB = 2048
N_SEQ = 16


def with_ends(values, rng, smallest, top_value):
    place = [jax.random.randint(jax.random.fold_in(rng, axis), (), 0, length) for axis, length in enumerate(values.shape)]
    widest = values.shape.index(max(values.shape))
    neighbour = place[:widest] + [(place[widest] + 1) % values.shape[widest]] + place[widest + 1:]
    return values.at[tuple(place)].set(smallest).at[tuple(neighbour)].set(top_value)


def block_levels(stream_key, dims, pieces, smallest, high):
    factor_of = 1.0
    for dim, blocks in pieces:
        steps = jax.random.uniform(jax.random.fold_in(jax.random.fold_in(stream_key, 6), dim), (blocks,), jnp.float32, smallest / len(pieces), high / len(pieces))
        factor_of = factor_of * jnp.repeat(jnp.exp(steps), dims[dim] // blocks).reshape((-1,) + (1,) * (len(dims) - 1 - dim))
    return factor_of


def scatter_about(key, dims, deviation, most, split=(), kind=jnp.bfloat16):
    drawn = deviation * jax.random.normal(key, dims, jnp.float32)
    if split:
        drawn = drawn * block_levels(key, dims, split, -0.22, 0.18)
    return jnp.clip(drawn, -most, most).astype(kind)


def setup_inputs(seed: int = 0, part: int = 0) -> dict:
    keys = jax.random.split(jax.random.key(seed), 8)
    part_splits = jax.random.split(jax.random.fold_in(keys[7], part), 8)
    student_rows = scatter_about(part_splits[0], (TOKENS, DS), 1.0, 6.0, ((0, 16),))
    teacher_rows = scatter_about(part_splits[1], (TOKENS, DT), 1.0, 6.0, ((0, 16),))
    student_head = scatter_about(keys[2], (VOCAB, DS), DS ** -0.5, 0.09375, ((0, 16),))
    teacher_head = scatter_about(keys[3], (VOCAB, DT), DT ** -0.5, 0.09375, ((0, 16),))
    student_lse = jnp.clip(0.5 + 2.0 * jax.random.uniform(part_splits[4], (TOKENS,), jnp.float32) ** block_levels(part_splits[4], (TOKENS,), ((0, 16),), -0.2, 0.2), 0.5, 2.5).astype(jnp.bfloat16)
    teacher_lse = jnp.clip(0.5 + 2.0 * jax.random.uniform(part_splits[5], (TOKENS,), jnp.float32) ** block_levels(part_splits[5], (TOKENS,), ((0, 16),), -0.2, 0.2), 0.5, 2.5).astype(jnp.bfloat16)
    targets = with_ends(jax.random.randint(part_splits[6], (TOKENS,), 0, VOCAB), jax.random.fold_in(part_splits[6], 1), 0, VOCAB - 1).astype(jnp.int32)
    return dict(student_rows=student_rows, teacher_rows=teacher_rows, student_head=student_head, teacher_head=teacher_head, student_lse=student_lse, teacher_lse=teacher_lse, targets=targets)


hard_weight = 0.5


def block_terms(student_block, teacher_block, student_norm, teacher_norm, target_block, student_panel, teacher_panel, panel):
    zs = jnp.dot(student_block, student_panel.T, preferred_element_type=jnp.float32)
    zt = jnp.dot(teacher_block, teacher_panel.T, preferred_element_type=jnp.float32)
    ls = zs - student_norm.astype(jnp.float32)[:, None]
    lt = zt - teacher_norm.astype(jnp.float32)[:, None]
    ps = jnp.exp(ls)
    pt = jnp.exp(lt)
    vocab_ids = panel * VP + jnp.arange(VP, dtype=jnp.int32)
    onehot = (target_block[:, None] == vocab_ids[None, :]).astype(jnp.float32)
    scores = ((1.0 + hard_weight) * ps - pt - hard_weight * onehot).astype(jnp.bfloat16)
    losses = jnp.sum(pt * (lt - ls) - hard_weight * onehot * ls, axis=1)
    rows_part = jnp.dot(scores, student_panel, preferred_element_type=jnp.float32)
    head_part = jnp.dot(scores.T, student_block, preferred_element_type=jnp.float32)
    return rows_part, losses, head_part


def reference(student_rows, teacher_rows, student_head, teacher_head, student_lse, teacher_lse, targets):
    student_blocks = student_rows.reshape(N_SEQ, TOK_DEV, DS)
    teacher_blocks = teacher_rows.reshape(N_SEQ, TOK_DEV, DT)
    student_norms = student_lse.reshape(N_SEQ, TOK_DEV)
    teacher_norms = teacher_lse.reshape(N_SEQ, TOK_DEV)
    target_blocks = targets.reshape(N_SEQ, TOK_DEV)
    student_panels = student_head.reshape(N_SEQ, VP, DS)
    teacher_panels = teacher_head.reshape(N_SEQ, VP, DT)
    block_ids = jnp.arange(N_SEQ, dtype=jnp.int32)
    rows_total = jnp.zeros((N_SEQ, TOK_DEV, DS), jnp.float32)
    loss_total = jnp.zeros((N_SEQ, TOK_DEV), jnp.float32)
    head_total = jnp.zeros((N_SEQ, VP, DS), jnp.bfloat16)
    for step in range(STEPS):
        panel_ids = ((block_ids - step) % N_SEQ).astype(jnp.int32)
        moved_student = jnp.roll(student_panels, step, axis=0)
        moved_teacher = jnp.roll(teacher_panels, step, axis=0)

        def one_block(items):
            return block_terms(*items)

        rows_part, losses, head_part = lax.map(one_block, (student_blocks, teacher_blocks, student_norms, teacher_norms, target_blocks, moved_student, moved_teacher, panel_ids))
        rows_total = rows_total + rows_part
        loss_total = loss_total + losses
        head_total = (head_total.astype(jnp.float32) + jnp.roll(head_part, -step, axis=0)).astype(jnp.bfloat16)
    return head_total.reshape(VOCAB, DS), rows_total.astype(jnp.bfloat16).reshape(TOKENS, DS), loss_total.reshape(TOKENS)
```

```python
import jax
import jax.numpy as jnp
from jax import lax
from jax.sharding import PartitionSpec as P

hard_weight = 0.5
CHUNKS = 4
STAGES = 2
BOTH = ("grp", "seq")


def permuted(value, move):
    groups, count = lax.axis_size("grp"), lax.axis_size("seq")
    pairs = []
    for group in range(groups):
        for place in range(count):
            to_group, to_place = move(group, place)
            pairs.append((group * count + place, to_group * count + to_place % count))
    return lax.ppermute(value, BOTH, pairs)


def next_chip(group, place):
    return group, place + 2


def previous_chip(group, place):
    return group, place - 2


def other_plane(group, place):
    return 1 - group, place


def other_core(group, place):
    return group, place + 1 - 2 * (place % 2)


def extra_out(group, place):
    return group, place + 1 + 2 * (place % 2)


def extra_back(group, place):
    return group, place - 3 + 2 * (place % 2)


def body(student_rows, teacher_rows, student_head, teacher_head, student_lse, teacher_lse, targets):
    count = lax.axis_size("seq")
    place = lax.axis_index("seq")
    plane = lax.axis_index("grp")
    core = place % 2
    width, depth = student_head.shape
    half = width // 2
    piece = half // CHUNKS
    student_norm = student_lse.astype(jnp.float32)[:, None]
    teacher_norm = teacher_lse.astype(jnp.float32)[:, None]

    def meeting(student_panel, teacher_panel, ids):
        zs = lax.dot_general(
            student_rows, student_panel, (((1,), (1,)), ((), ())), preferred_element_type=jnp.float32
        )
        zt = lax.dot_general(
            teacher_rows, teacher_panel, (((1,), (1,)), ((), ())), preferred_element_type=jnp.float32
        )
        ls = zs - student_norm
        lt = zt - teacher_norm
        ps = jnp.exp(ls)
        pt = jnp.exp(lt)
        onehot = (targets[:, None] == ids[None, :]).astype(jnp.float32)
        scores = ((1.0 + hard_weight) * ps - pt - hard_weight * onehot).astype(jnp.bfloat16)
        losses = jnp.sum(pt * (lt - ls) - hard_weight * onehot * ls, axis=1)
        part = lax.dot_general(
            scores, student_rows, (((0,), (0,)), ((), ())), preferred_element_type=jnp.float32
        )
        return scores, losses, part

    mine_rows = lax.dynamic_slice_in_dim(student_head, plane * half, half, 0)
    mine_rows_t = lax.dynamic_slice_in_dim(teacher_head, plane * half, half, 0)
    crossed = []
    for k in range(CHUNKS):
        lo, hi = k * piece, (k + 1) * piece
        chunk = jnp.concatenate([mine_rows[lo:hi], mine_rows_t[lo:hi]], axis=1)
        crossed.append(permuted(chunk, next_chip))
    swapped = [permuted(chunk, other_plane) for chunk in crossed]

    whole, _ = lax.optimization_barrier((jnp.concatenate([student_head, teacher_head], axis=1), crossed[-1]))
    extra = permuted(whole, extra_out)

    ids_in = jnp.arange(width, dtype=jnp.int32)
    own_scores, losses, own_part = meeting(student_head, teacher_head, place * width + ids_in)
    loss_total = losses
    score_list, panel_list = [own_scores], [student_head]

    per_stage = CHUNKS // STAGES
    near = (place - 2) % count
    far = (place - 1 - 2 * core) % count
    mine_parts, other_parts = [], []
    for stage in range(STAGES):
        picks = range(stage * per_stage, (stage + 1) * per_stage)
        mine = jnp.concatenate([crossed[k] for k in picks] + [swapped[k] for k in picks], axis=0)
        theirs = permuted(mine, other_core)
        both = jnp.concatenate([mine, theirs], axis=0)
        rows = jnp.arange(per_stage * piece, dtype=jnp.int32) + stage * per_stage * piece
        inside = jnp.concatenate([plane * half + rows, (1 - plane) * half + rows])
        ids = jnp.concatenate([near * width + inside, far * width + inside])
        scores, losses, part = meeting(both[:, :depth], both[:, depth:], ids)
        loss_total = loss_total + losses
        score_list.append(scores)
        panel_list.append(both[:, :depth])
        keep, give = part[: mine.shape[0]], part[mine.shape[0] :]
        got = permuted(give.astype(jnp.bfloat16), other_core)
        total = (keep + got.astype(jnp.float32)).astype(jnp.bfloat16)
        back = permuted(total, previous_chip)
        mine_parts.append(back[: per_stage * piece])
        other_parts.append(back[per_stage * piece :])

    extra_id = jnp.where(core == 1, place - 1, place - 3) % count
    scores, losses, part = meeting(extra[:, :depth], extra[:, depth:], extra_id * width + ids_in)
    loss_total = loss_total + losses
    score_list.append(scores)
    panel_list.append(extra[:, :depth])
    extra_part = permuted(part.astype(jnp.bfloat16), extra_back)

    rows_grad = jnp.dot(
        jnp.concatenate(score_list, axis=1),
        jnp.concatenate(panel_list, axis=0),
        preferred_element_type=jnp.float32,
    ).astype(jnp.bfloat16)

    mine_parts = jnp.concatenate(mine_parts, axis=0)
    other_parts = jnp.concatenate(other_parts, axis=0)
    first = jnp.where(plane == 0, mine_parts, other_parts)
    second = jnp.where(plane == 0, other_parts, mine_parts)
    from_next = jnp.concatenate([first, second], axis=0)
    head_grad = (
        own_part + from_next.astype(jnp.float32) + extra_part.astype(jnp.float32)
    ).astype(jnp.bfloat16)
    return (head_grad, rows_grad, loss_total)


def solution(mesh):
    placed = (
        P(("grp", "seq"), None),
        P(("grp", "seq"), None),
        P("seq", None),
        P("seq", None),
        P(("grp", "seq")),
        P(("grp", "seq")),
        P(("grp", "seq")),
    )
    return jax.shard_map(
        body,
        mesh=mesh,
        in_specs=placed,
        out_specs=(P(("grp", "seq"), None), P(("grp", "seq"), None), P(("grp", "seq"))),
        check_vma=False,
    )
```

```python
import jax
import jax.numpy as jnp
from jax import lax
from jax.experimental import pallas as pl
from jax.sharding import PartitionSpec as P

hard_weight = 0.5
CHUNKS = 4
BOTH = ("grp", "seq")


def permuted(value, move):
    groups, count = lax.axis_size("grp"), lax.axis_size("seq")
    pairs = []
    for group in range(groups):
        for place in range(count):
            to_group, to_place = move(group, place)
            pairs.append((group * count + place, to_group * count + to_place % count))
    return lax.ppermute(value, BOTH, pairs)


def next_chip(group, place):
    return group, place + 2


def previous_chip(group, place):
    return group, place - 2


def other_plane(group, place):
    return 1 - group, place


def other_core(group, place):
    return group, place + 1 - 2 * (place % 2)


def extra_out(group, place):
    return group, place + 1 + 2 * (place % 2)


def extra_back(group, place):
    return group, place - 3 + 2 * (place % 2)


def gate(values, ready):
    operands = list(values) + list(ready)
    anywhere = pl.BlockSpec(memory_space=pl.ANY)
    return pl.pallas_call(
        lambda *refs: None,
        out_shape=[jax.ShapeDtypeStruct(value.shape, value.dtype) for value in values],
        in_specs=[anywhere] * len(operands),
        out_specs=[anywhere] * len(values),
        input_output_aliases={index: index for index in range(len(values))},
    )(*operands)


def body(student_rows, teacher_rows, student_head, teacher_head, student_lse, teacher_lse, targets):
    count = lax.axis_size("seq")
    place = lax.axis_index("seq")
    plane = lax.axis_index("grp")
    core = place % 2
    width, depth = student_head.shape
    half = width // 2
    piece = half // CHUNKS
    student_norm = student_lse.astype(jnp.float32)
    teacher_norm = teacher_lse.astype(jnp.float32)

    def logits(rows, panel, norm):
        return lax.dot_general(
            rows, panel, (((1,), (1,)), ((), ())), preferred_element_type=jnp.float32
        ) - norm[:, None]

    def terms(ls, lt, ids):
        ps = jnp.exp(ls)
        pt = jnp.exp(lt)
        onehot = (targets[:, None] == ids[None, :]).astype(jnp.float32)
        scores = ((1.0 + hard_weight) * ps - pt - hard_weight * onehot).astype(jnp.bfloat16)
        losses = jnp.sum(pt * (lt - ls) - hard_weight * onehot * ls, axis=1)
        return scores, losses

    def head_part(scores):
        return lax.dot_general(
            scores, student_rows, (((0,), (0,)), ((), ())), preferred_element_type=jnp.float32
        )

    def chunk(k):
        at = plane * half + k * piece
        return jnp.concatenate(
            [
                lax.dynamic_slice_in_dim(student_head, at, piece, 0),
                lax.dynamic_slice_in_dim(teacher_head, at, piece, 0),
            ],
            axis=1,
        )

    def own_half(k):
        lo, hi = k * half, (k + 1) * half
        return jnp.concatenate([student_head[lo:hi], teacher_head[lo:hi]], axis=1)

    ids_in = jnp.arange(width, dtype=jnp.int32)
    chunks = [chunk(k) for k in range(CHUNKS)]
    sends = [own_half(0), own_half(1)]

    crossed = [permuted(chunks[0], next_chip), permuted(chunks[1], next_chip), None, None]
    crossed[0], chunks[2], norm = gate([crossed[0], chunks[2], student_norm], [])
    swapped = [permuted(crossed[0], other_plane), None, None, None]
    crossed[2] = permuted(chunks[2], next_chip)
    ls = logits(student_rows, student_head, norm)
    crossed[1], chunks[3], norm = gate([crossed[1], chunks[3], teacher_norm], [ls])
    swapped[1] = permuted(crossed[1], other_plane)
    crossed[3] = permuted(chunks[3], next_chip)
    lt = logits(teacher_rows, teacher_head, norm)
    own_scores, losses = terms(ls, lt, place * width + ids_in)
    loss_total = losses
    score_list, panel_list = [], []
    crossed[2], sends[0], own_scores = gate([crossed[2], sends[0], own_scores], [])
    swapped[2] = permuted(crossed[2], other_plane)
    extra = [permuted(sends[0], extra_out), None]

    near = (place - 2) % count
    far = (place - 1 - 2 * core) % count

    def stage_ids(stage):
        rows = jnp.arange(half // 2, dtype=jnp.int32) + stage * (half // 2)
        inside = jnp.concatenate([plane * half + rows, (1 - plane) * half + rows])
        return jnp.concatenate([near * width + inside, far * width + inside])

    def stage_terms(stage, mine, theirs, norm, norm_t):
        both = jnp.concatenate([mine, theirs], axis=0)
        panel = both[:, :depth]
        scores, losses = terms(
            logits(student_rows, panel, norm), logits(teacher_rows, both[:, depth:], norm_t), stage_ids(stage)
        )
        part = head_part(scores)
        return panel, scores, losses, part[:half], part[half:].astype(jnp.bfloat16)

    mine0 = jnp.concatenate([crossed[0], crossed[1], swapped[0], swapped[1]], axis=0)
    mine0, own_scores = gate([mine0, own_scores], [])
    theirs0 = permuted(mine0, other_core)
    own_part = head_part(own_scores)
    score_list.append(own_scores)
    panel_list.append(student_head)
    crossed[3], = gate([crossed[3]], [own_part])
    swapped[3] = permuted(crossed[3], other_plane)
    theirs0, norm, norm_t = gate([theirs0, student_norm, teacher_norm], [])
    panel, scores, losses, keep, give = stage_terms(0, mine0, theirs0, norm, norm_t)
    loss_total = loss_total + losses
    score_list.append(scores)
    panel_list.append(panel)
    got = permuted(give, other_core)
    total = (keep + got.astype(jnp.float32)).astype(jnp.bfloat16)
    back0 = permuted(total, previous_chip)

    swapped[2], swapped[3], sends[1] = gate([swapped[2], swapped[3], sends[1]], [total])
    mine1 = jnp.concatenate([crossed[2], crossed[3], swapped[2], swapped[3]], axis=0)
    theirs1 = permuted(mine1, other_core)
    extra[1] = permuted(sends[1], extra_out)
    theirs1, norm, norm_t = gate([theirs1, student_norm, teacher_norm], [])
    panel, scores, losses, keep, give = stage_terms(1, mine1, theirs1, norm, norm_t)
    loss_total = loss_total + losses
    score_list.append(scores)
    panel_list.append(panel)
    got = permuted(give, other_core)

    extra_id = jnp.where(core == 1, place - 1, place - 3) % count
    extra_parts = []

    def extra_terms(k, value, norm, norm_t):
        ids = extra_id * width + k * half + jnp.arange(half, dtype=jnp.int32)
        scores, losses = terms(
            logits(student_rows, value[:, :depth], norm), logits(teacher_rows, value[:, depth:], norm_t), ids
        )
        return scores, losses, head_part(scores).astype(jnp.bfloat16)

    value, norm, norm_t = gate([extra[0], student_norm, teacher_norm], [give])
    scores, losses, part = extra_terms(0, value, norm, norm_t)
    loss_total = loss_total + losses
    score_list.append(scores)
    panel_list.append(value[:, :depth])
    total = (keep + got.astype(jnp.float32)).astype(jnp.bfloat16)
    total, part = gate([total, part], [])
    back1 = permuted(total, previous_chip)
    extra_parts.append(permuted(part, extra_back))

    value, norm, norm_t = gate([extra[1], student_norm, teacher_norm], [total])
    scores, losses, part = extra_terms(1, value, norm, norm_t)
    loss_total = loss_total + losses
    score_list.append(scores)
    panel_list.append(value[:, :depth])
    part, scores = gate([part, scores], [])
    extra_parts.append(permuted(part, extra_back))
    score_list[-1] = scores

    rows_grad = jnp.dot(
        jnp.concatenate(score_list, axis=1),
        jnp.concatenate(panel_list, axis=0),
        preferred_element_type=jnp.float32,
    ).astype(jnp.bfloat16)

    quarter = half // 2
    mine_parts = jnp.concatenate([back0[:quarter], back1[:quarter]], axis=0)
    other_parts = jnp.concatenate([back0[quarter:], back1[quarter:]], axis=0)
    first = jnp.where(plane == 0, mine_parts, other_parts)
    second = jnp.where(plane == 0, other_parts, mine_parts)
    from_next = jnp.concatenate([first, second], axis=0)
    extra_part = jnp.concatenate(extra_parts, axis=0)
    head_grad = (
        own_part + from_next.astype(jnp.float32) + extra_part.astype(jnp.float32)
    ).astype(jnp.bfloat16)
    return (head_grad, rows_grad, loss_total)


def solution(mesh):
    placed = (
        P(("grp", "seq"), None),
        P(("grp", "seq"), None),
        P("seq", None),
        P("seq", None),
        P(("grp", "seq")),
        P(("grp", "seq")),
        P(("grp", "seq")),
    )
    return jax.shard_map(
        body,
        mesh=mesh,
        in_specs=placed,
        out_specs=(P(("grp", "seq"), None), P(("grp", "seq"), None), P(("grp", "seq"))),
        check_vma=False,
    )
```

```python
import jax
import jax.numpy as jnp
from jax import lax
from jax.experimental import pallas as pl
from jax.experimental.pallas import tpu as pltpu
from jax.sharding import PartitionSpec as P

hard_weight = 0.5
CHUNKS = 4
GATE_VMEM = 128 * 1024
BOTH = ("grp", "seq")


def permuted(value, move):
    groups, count = lax.axis_size("grp"), lax.axis_size("seq")
    pairs = []
    for group in range(groups):
        for place in range(count):
            to_group, to_place = move(group, place)
            pairs.append((group * count + place, to_group * count + to_place % count))
    return lax.ppermute(value, BOTH, pairs)


def next_chip(group, place):
    return group, place + 2


def previous_chip(group, place):
    return group, place - 2


def other_plane(group, place):
    return 1 - group, place


def other_core(group, place):
    return group, place + 1 - 2 * (place % 2)


def extra_out(group, place):
    return group, place + 1 + 2 * (place % 2)


def extra_back(group, place):
    return group, place - 3 + 2 * (place % 2)


def gate(values, ready):
    operands = list(values) + list(ready)
    anywhere = pl.BlockSpec(memory_space=pl.ANY)
    return pl.pallas_call(
        lambda *refs: None,
        out_shape=[jax.ShapeDtypeStruct(value.shape, value.dtype) for value in values],
        in_specs=[anywhere] * len(operands),
        out_specs=[anywhere] * len(values),
        input_output_aliases={index: index for index in range(len(values))},
        compiler_params=pltpu.CompilerParams(vmem_limit_bytes=GATE_VMEM),
        cost_estimate=pl.CostEstimate(flops=0, bytes_accessed=0, transcendentals=0),
    )(*operands)


def body(student_rows, teacher_rows, student_head, teacher_head, student_lse, teacher_lse, targets):
    count = lax.axis_size("seq")
    place = lax.axis_index("seq")
    plane = lax.axis_index("grp")
    core = place % 2
    width, depth = student_head.shape
    half = width // 2
    piece = half // CHUNKS
    student_norm = student_lse.astype(jnp.float32)
    teacher_norm = teacher_lse.astype(jnp.float32)

    def logits(rows, panel, norm):
        return lax.dot_general(
            rows, panel, (((1,), (1,)), ((), ())), preferred_element_type=jnp.float32
        ) - norm[:, None]

    def terms(ls, lt, ids):
        ps = jnp.exp(ls)
        pt = jnp.exp(lt)
        onehot = (targets[:, None] == ids[None, :]).astype(jnp.float32)
        scores = ((1.0 + hard_weight) * ps - pt - hard_weight * onehot).astype(jnp.bfloat16)
        losses = jnp.sum(pt * (lt - ls) - hard_weight * onehot * ls, axis=1)
        return scores, losses

    def head_part(scores):
        return lax.dot_general(
            scores, student_rows, (((0,), (0,)), ((), ())), preferred_element_type=jnp.float32
        )

    def chunk(k):
        at = plane * half + k * piece
        return jnp.concatenate(
            [
                lax.dynamic_slice_in_dim(student_head, at, piece, 0),
                lax.dynamic_slice_in_dim(teacher_head, at, piece, 0),
            ],
            axis=1,
        )

    def own_half(k):
        lo, hi = k * half, (k + 1) * half
        return jnp.concatenate([student_head[lo:hi], teacher_head[lo:hi]], axis=1)

    ids_in = jnp.arange(width, dtype=jnp.int32)
    chunks = [chunk(k) for k in range(CHUNKS)]
    sends = [own_half(0), own_half(1)]

    crossed = [permuted(chunks[0], next_chip), permuted(chunks[1], next_chip), None, None]
    crossed[0], chunks[2], norm = gate([crossed[0], chunks[2], student_norm], [])
    swapped = [permuted(crossed[0], other_plane), None, None, None]
    crossed[2] = permuted(chunks[2], next_chip)
    ls = logits(student_rows, student_head, norm)
    crossed[1], chunks[3], norm_t = gate([crossed[1], chunks[3], teacher_norm], [ls])
    swapped[1] = permuted(crossed[1], other_plane)
    crossed[3] = permuted(chunks[3], next_chip)
    lt = logits(teacher_rows, teacher_head, norm_t)
    own_scores, losses = terms(ls, lt, place * width + ids_in)
    loss_total = losses
    score_list, panel_list = [], []
    crossed[2], sends[0], own_scores = gate([crossed[2], sends[0], own_scores], [])
    swapped[2] = permuted(crossed[2], other_plane)
    extra = [permuted(sends[0], extra_out), None]

    near = (place - 2) % count
    far = (place - 1 - 2 * core) % count

    def stage_ids(stage):
        rows = jnp.arange(half // 2, dtype=jnp.int32) + stage * (half // 2)
        inside = jnp.concatenate([plane * half + rows, (1 - plane) * half + rows])
        return jnp.concatenate([near * width + inside, far * width + inside])

    def stage_terms(stage, mine, theirs, norm, norm_t):
        both = jnp.concatenate([mine, theirs], axis=0)
        panel = both[:, :depth]
        scores, losses = terms(
            logits(student_rows, panel, norm), logits(teacher_rows, both[:, depth:], norm_t), stage_ids(stage)
        )
        part = head_part(scores)
        return panel, scores, losses, part[:half], part[half:].astype(jnp.bfloat16)

    mine0 = jnp.concatenate([crossed[0], crossed[1], swapped[0], swapped[1]], axis=0)
    mine0, own_scores = gate([mine0, own_scores], [])
    theirs0 = permuted(mine0, other_core)
    own_part = head_part(own_scores)
    score_list.append(own_scores)
    panel_list.append(student_head)
    crossed[3], = gate([crossed[3]], [own_part])
    swapped[3] = permuted(crossed[3], other_plane)
    theirs0, norm, norm_t = gate([theirs0, norm, norm_t], [])
    panel, scores, losses, keep, give = stage_terms(0, mine0, theirs0, norm, norm_t)
    loss_total = loss_total + losses
    score_list.append(scores)
    panel_list.append(panel)
    got = permuted(give, other_core)
    total = (keep + got.astype(jnp.float32)).astype(jnp.bfloat16)
    back0 = permuted(total, previous_chip)

    swapped[2], swapped[3], sends[1] = gate([swapped[2], swapped[3], sends[1]], [total])
    mine1 = jnp.concatenate([crossed[2], crossed[3], swapped[2], swapped[3]], axis=0)
    theirs1 = permuted(mine1, other_core)
    extra[1] = permuted(sends[1], extra_out)
    theirs1, norm, norm_t = gate([theirs1, norm, norm_t], [])
    panel, scores, losses, keep, give = stage_terms(1, mine1, theirs1, norm, norm_t)
    loss_total = loss_total + losses
    score_list.append(scores)
    panel_list.append(panel)
    got = permuted(give, other_core)

    extra_id = jnp.where(core == 1, place - 1, place - 3) % count
    extra_parts = []

    def extra_terms(k, value, norm, norm_t):
        ids = extra_id * width + k * half + jnp.arange(half, dtype=jnp.int32)
        scores, losses = terms(
            logits(student_rows, value[:, :depth], norm), logits(teacher_rows, value[:, depth:], norm_t), ids
        )
        return scores, losses, head_part(scores).astype(jnp.bfloat16)

    value, norm, norm_t = gate([extra[0], norm, norm_t], [give])
    scores, losses, part = extra_terms(0, value, norm, norm_t)
    loss_total = loss_total + losses
    score_list.append(scores)
    panel_list.append(value[:, :depth])
    total = (keep + got.astype(jnp.float32)).astype(jnp.bfloat16)
    total, part = gate([total, part], [])
    back1 = permuted(total, previous_chip)
    extra_parts.append(permuted(part, extra_back))

    value, norm, norm_t = gate([extra[1], norm, norm_t], [total])
    scores, losses, part = extra_terms(1, value, norm, norm_t)
    loss_total = loss_total + losses
    score_list.append(scores)
    panel_list.append(value[:, :depth])
    part, scores = gate([part, scores], [])
    extra_parts.append(permuted(part, extra_back))
    score_list[-1] = scores

    rows_grad = jnp.dot(
        jnp.concatenate(score_list, axis=1),
        jnp.concatenate(panel_list, axis=0),
        preferred_element_type=jnp.float32,
    ).astype(jnp.bfloat16)

    quarter = half // 2
    back0, back1 = gate([back0, back1], [part])
    mine_parts = jnp.concatenate([back0[:quarter], back1[:quarter]], axis=0)
    other_parts = jnp.concatenate([back0[quarter:], back1[quarter:]], axis=0)
    first = jnp.where(plane == 0, mine_parts, other_parts)
    second = jnp.where(plane == 0, other_parts, mine_parts)
    from_next = jnp.concatenate([first, second], axis=0)
    extra_part = jnp.concatenate(extra_parts, axis=0)
    head_grad = (
        own_part + from_next.astype(jnp.float32) + extra_part.astype(jnp.float32)
    ).astype(jnp.bfloat16)
    return (head_grad, rows_grad, loss_total)


def solution(mesh):
    placed = (
        P(("grp", "seq"), None),
        P(("grp", "seq"), None),
        P("seq", None),
        P("seq", None),
        P(("grp", "seq")),
        P(("grp", "seq")),
        P(("grp", "seq")),
    )
    return jax.shard_map(
        body,
        mesh=mesh,
        in_specs=placed,
        out_specs=(P(("grp", "seq"), None), P(("grp", "seq"), None), P(("grp", "seq"))),
        check_vma=False,
    )
```

```python
import jax
import jax.numpy as jnp
from jax import lax
from jax.experimental import pallas as pl
from jax.experimental.pallas import tpu as pltpu
from jax.sharding import PartitionSpec as P

hard_weight = 0.5
CHUNKS = 4
GATE_VMEM = 128 * 1024
BOTH = ("grp", "seq")


def permuted(value, move):
    groups, count = lax.axis_size("grp"), lax.axis_size("seq")
    pairs = []
    for group in range(groups):
        for place in range(count):
            target = move(group, place)
            if target is not None:
                pairs.append((group * count + place, target[0] * count + target[1] % count))
    return lax.ppermute(value, BOTH, pairs)


def next_chip(group, place):
    return group, place + 2


def previous_chip(group, place):
    return group, place - 2


def other_plane(group, place):
    return 1 - group, place


def other_core(group, place):
    return group, place + 1 - 2 * (place % 2)


def extra_early(group, place):
    if place % 2 == 0:
        return group, place + 1
    return (group, place + 3) if place // 2 % 2 == 0 else None


def extra_late(group, place):
    return (group, place + 3) if place % 2 == 1 and place // 2 % 2 == 1 else None


def extra_back(group, place):
    return group, place - 3 + 2 * (place % 2)


def gate(values, ready, flops=0):
    operands = list(values) + list(ready)
    anywhere = pl.BlockSpec(memory_space=pl.ANY)
    return pl.pallas_call(
        lambda *refs: None,
        out_shape=[jax.ShapeDtypeStruct(value.shape, value.dtype) for value in values],
        in_specs=[anywhere] * len(operands),
        out_specs=[anywhere] * len(values),
        input_output_aliases={index: index for index in range(len(values))},
        compiler_params=pltpu.CompilerParams(vmem_limit_bytes=GATE_VMEM),
        cost_estimate=pl.CostEstimate(flops=flops, bytes_accessed=0, transcendentals=0),
    )(*operands)


def packed(at, student_head, teacher_head, places, ready=()):
    depth, depth_t = student_head.shape[1], teacher_head.shape[1]

    def kernel(at_ref, student_ref, teacher_ref, *refs):
        outs, sems = refs[len(ready) : -1], refs[-1]
        copies = []
        for index, (moves, start, rows) in enumerate(places):
            first = pl.multiple_of(at_ref[0] + start, 16) if moves else start
            for half, (source, lo, wide) in enumerate(
                [(student_ref, 0, depth), (teacher_ref, depth, depth_t)]
            ):
                copies.append(
                    pltpu.make_async_copy(
                        source.at[pl.ds(first, rows), :],
                        outs[index].at[:, pl.ds(lo, wide)],
                        sems.at[2 * index + half],
                    )
                )
        for copy in copies:
            copy.start()
        for copy in copies:
            copy.wait()

    anywhere = pl.BlockSpec(memory_space=pl.ANY)
    return pl.pallas_call(
        kernel,
        out_shape=[
            jax.ShapeDtypeStruct((rows, depth + depth_t), student_head.dtype) for _, _, rows in places
        ],
        in_specs=[pl.BlockSpec(memory_space=pltpu.SMEM)]
        + [pl.BlockSpec(memory_space=pltpu.HBM)] * 2
        + [anywhere] * len(ready),
        out_specs=[anywhere] * len(places),
        scratch_shapes=[pltpu.SemaphoreType.DMA((2 * len(places),))],
        compiler_params=pltpu.CompilerParams(vmem_limit_bytes=GATE_VMEM),
    )(at, student_head, teacher_head, *ready)


def head_total(at, own_part, backs, extras):
    width, depth = own_part.shape
    half = width // 2
    quarter = half // 2
    block = depth // 4

    def kernel(at_ref, own_ref, back0, back1, extra0, extra1, out_ref):
        for side in range(2):
            base = at_ref[0] if side == 0 else half - at_ref[0]
            low = base == 0
            for stage, back in enumerate((back0, back1)):
                rows = pl.ds(pl.multiple_of(base + stage * quarter, quarter), quarter)
                picked = pl.ds(stage * quarter, quarter)
                upper = extra0[pl.ds(half, quarter), :] if stage == 0 else extra1[...]
                extra = jnp.where(low, extra0[picked, :], upper)
                out_ref[rows, :] = (
                    own_ref[rows, :]
                    + back[pl.ds(side * quarter, quarter), :].astype(jnp.float32)
                    + extra.astype(jnp.float32)
                ).astype(out_ref.dtype)

    def columns(rows):
        return pl.BlockSpec((rows, block), lambda index: (0, index))

    return pl.pallas_call(
        kernel,
        grid=(4,),
        out_shape=jax.ShapeDtypeStruct((width, depth), jnp.bfloat16),
        in_specs=[pl.BlockSpec(memory_space=pltpu.SMEM), columns(width)]
        + [columns(half)] * 2
        + [columns(extra.shape[0]) for extra in extras],
        out_specs=columns(width),
        compiler_params=pltpu.CompilerParams(vmem_limit_bytes=8 * 1024 * 1024),
    )(at, own_part, *backs, *extras)


def pause(order, ready):
    return gate([order], ready, 30_000_000_000)[0]


def free():
    return pl.CostEstimate(flops=0, bytes_accessed=0, transcendentals=0)


def meeting(rows_s, rows_t, panels, panels_t, norm, norm_t, targets, ids, loss, kinds, ready=()):
    count, depth = rows_s.shape
    depth_t = rows_t.shape[1]
    pieces = len(panels)
    width = sum(panel.shape[0] for panel in panels)
    block = count // 2
    part_rows = width // len(kinds)
    whole = pl.BlockSpec(memory_space=pltpu.VMEM)
    contract = (((1,), (1,)), ((), ()))

    def kernel(*refs):
        s_ref, t_ref, norm_ref, norm_t_ref, target_ref, ids_ref, loss_in = refs[:7]
        panel_refs = refs[7 : 7 + pieces]
        panel_t_refs = refs[7 + pieces : 7 + 2 * pieces]
        score_ref, loss_ref = refs[7 + 2 * pieces + len(ready) :][:2]
        part_refs = refs[9 + 2 * pieces + len(ready) :]
        panel = jnp.concatenate([ref[:, :depth] for ref in panel_refs], axis=0)
        panel_t = jnp.concatenate([ref[:, ref.shape[1] - depth_t :] for ref in panel_t_refs], axis=0)

        @pl.loop(0, 2)
        def _(step):
            rows = pl.ds(pl.multiple_of(step * block, block), block)
            zs = lax.dot_general(s_ref[rows, :], panel, contract, preferred_element_type=jnp.float32)
            zt = lax.dot_general(t_ref[rows, :], panel_t, contract, preferred_element_type=jnp.float32)
            ls = zs - norm_ref[rows, :]
            lt = zt - norm_t_ref[rows, :]
            ps = jnp.exp(ls)
            pt = jnp.exp(lt)
            onehot = (target_ref[rows, :] == ids_ref[...]).astype(jnp.float32)
            scores = ((1.0 + hard_weight) * ps - pt - hard_weight * onehot).astype(jnp.bfloat16)
            score_ref[rows, :] = scores
            loss_ref[rows, :] = loss_in[rows, :] + jnp.sum(
                pt * (lt - ls) - hard_weight * onehot * ls, axis=1, keepdims=True
            )

        part = lax.dot_general(
            score_ref[...], s_ref[...], (((0,), (0,)), ((), ())), preferred_element_type=jnp.float32
        )
        for index, part_ref in enumerate(part_refs):
            part_ref[...] = part[index * part_rows : (index + 1) * part_rows].astype(part_ref.dtype)

    return pl.pallas_call(
        kernel,
        out_shape=[
            jax.ShapeDtypeStruct((count, width), jnp.bfloat16),
            jax.ShapeDtypeStruct((count, 1), jnp.float32),
        ]
        + [jax.ShapeDtypeStruct((part_rows, depth), kind) for kind in kinds],
        in_specs=[whole] * (7 + 2 * pieces) + [pl.BlockSpec(memory_space=pl.ANY)] * len(ready),
        out_specs=[whole] * (2 + len(kinds)),
        compiler_params=pltpu.CompilerParams(vmem_limit_bytes=16 * 1024 * 1024),
        cost_estimate=free(),
    )(rows_s, rows_t, norm, norm_t, targets, ids, loss, *panels, *panels_t, *ready)


def rows_product(scores, panels, depth, ready):
    count = scores[0].shape[0]
    block = depth // 7
    inner = sum(panel.shape[0] for panel in panels)
    whole = pl.BlockSpec(memory_space=pltpu.VMEM)

    def kernel(*refs):
        score_refs = refs[: len(scores)]
        panel_refs = refs[len(scores) : len(scores) + len(panels)]
        out_ref, left_ref = refs[-2:]

        @pl.when(pl.program_id(0) == 0)
        def _():
            left_ref[...] = jnp.concatenate([ref[...] for ref in score_refs], axis=1)

        right = jnp.concatenate([ref[...] for ref in panel_refs], axis=0)
        out_ref[...] = jnp.dot(
            left_ref[...], right, preferred_element_type=jnp.float32
        ).astype(out_ref.dtype)

    return pl.pallas_call(
        kernel,
        grid=(7,),
        out_shape=jax.ShapeDtypeStruct((count, depth), jnp.bfloat16),
        in_specs=[whole] * len(scores)
        + [pl.BlockSpec((panel.shape[0], block), lambda index: (0, index)) for panel in panels]
        + [pl.BlockSpec(memory_space=pl.ANY)] * len(ready),
        out_specs=pl.BlockSpec((count, block), lambda index: (0, index)),
        scratch_shapes=[pltpu.VMEM((count, inner), jnp.bfloat16)],
        compiler_params=pltpu.CompilerParams(vmem_limit_bytes=16 * 1024 * 1024),
        cost_estimate=free(),
    )(*scores, *panels, *ready)


def body(student_rows, teacher_rows, student_head, teacher_head, student_lse, teacher_lse, targets):
    count = lax.axis_size("seq")
    place = lax.axis_index("seq")
    plane = lax.axis_index("grp")
    core = place % 2
    width, depth = student_head.shape
    half = width // 2
    quarter = half // 2
    piece = half // CHUNKS
    norm = student_lse.astype(jnp.float32)[:, None]
    norm_t = teacher_lse.astype(jnp.float32)[:, None]
    wanted = targets[:, None]
    order = jnp.zeros((8, 128), jnp.float32)
    ids_in = jnp.arange(width, dtype=jnp.int32)
    near = (place - 2) % count
    far = (place - 1 - 2 * core) % count
    extra_id = jnp.where(core == 1, place - 1, place - 3) % count
    from_late = jnp.logical_and(core == 0, place // 2 % 2 == 1)

    def stage_ids(stage):
        rows = jnp.arange(half // 2, dtype=jnp.int32) + stage * (half // 2)
        inside = jnp.concatenate([plane * half + rows, (1 - plane) * half + rows])
        return jnp.concatenate([near * width + inside, far * width + inside])

    def meet(panels, panels_t, ids, loss, kinds, ready):
        return meeting(
            student_rows, teacher_rows, panels, panels_t, norm, norm_t, wanted, ids[None, :], loss, kinds, ready
        )

    at = jnp.reshape(plane * half, (1,)).astype(jnp.int32)
    chunks = packed(at, student_head, teacher_head, [(True, k * piece, piece) for k in range(2)])
    chunks = list(chunks)
    chunks += packed(
        at,
        student_head,
        teacher_head,
        [(True, k * piece, piece) for k in range(2, 4)] + [(False, 0, width)],
    )
    send = chunks.pop()

    crossed = [permuted(chunks[0], next_chip), permuted(chunks[1], next_chip), None, None]
    early = permuted(send, extra_early)
    swapped = [None] * 4
    order = pause(order, [chunks[0]])
    crossed[0], chunks[2], order = gate([crossed[0], chunks[2], order], [])
    swapped[0] = permuted(crossed[0], other_plane)
    crossed[2] = permuted(chunks[2], next_chip)
    own_scores, loss, own_part = meet(
        [student_head],
        [teacher_head],
        place * width + ids_in,
        jnp.zeros_like(norm),
        [jnp.float32],
        [order],
    )
    crossed[1], chunks[3], order = gate([crossed[1], chunks[3], order], [own_scores])
    swapped[1] = permuted(crossed[1], other_plane)
    crossed[3] = permuted(chunks[3], next_chip)
    order = pause(order, [])
    crossed[2], order = gate([crossed[2], order], [])
    swapped[2] = permuted(crossed[2], other_plane)
    send, = packed(at, student_head, teacher_head, [(False, 0, width - quarter)], [order])
    late = [permuted(send, extra_late), None]
    order = pause(order, [])
    swapped[0], swapped[1], order = gate([swapped[0], swapped[1], order], [])
    mine0 = jnp.concatenate([crossed[0], crossed[1], swapped[0], swapped[1]], axis=0)
    theirs0 = permuted(mine0, other_core)
    order = pause(order, [mine0])
    crossed[3], order = gate([crossed[3], order], [])
    swapped[3] = permuted(crossed[3], other_plane)

    order = pause(order, [])
    theirs0, early, order = gate([theirs0, early, order], [])
    pair = [mine0, theirs0]
    scores0, loss, keep, give = meet(pair, pair, stage_ids(0), loss, [jnp.float32, jnp.bfloat16], [order])
    got = permuted(give, other_core)
    order = pause(order, [give])
    got, order = gate([got, order], [])
    total = (keep + got.astype(jnp.float32)).astype(jnp.bfloat16)
    back0 = permuted(total, previous_chip)

    swapped[2], swapped[3], order = gate([swapped[2], swapped[3], order], [total])
    mine1 = jnp.concatenate([crossed[2], crossed[3], swapped[2], swapped[3]], axis=0)
    theirs1 = permuted(mine1, other_core)
    send, = packed(at, student_head, teacher_head, [(False, width - quarter, quarter)], [order])
    late[1] = permuted(send, extra_late)
    order = pause(order, [mine1])
    theirs1, order = gate([theirs1, order], [])
    pair = [mine1, theirs1]
    scores1, loss, keep, give = meet(pair, pair, stage_ids(1), loss, [jnp.float32, jnp.bfloat16], [order])
    got = permuted(give, other_core)
    order = pause(order, [give])
    got, order = gate([got, order], [])
    total = (keep + got.astype(jnp.float32)).astype(jnp.bfloat16)
    back1 = permuted(total, previous_chip)

    extra_parts, extra_scores, extras = [], [], []
    last = total
    for k in range(2):
        order = pause(order, [last])
        late[k], order = gate([late[k], order], [])
        lo, hi = (0, width - quarter) if k == 0 else (width - quarter, width)
        value = jnp.where(from_late, late[k], early[lo:hi])
        ids = extra_id * width + ids_in[lo:hi]
        scores, loss, last = meet([value], [value], ids, loss, [jnp.bfloat16], [order])
        extra_parts.append(permuted(last, extra_back))
        extra_scores.append(scores)
        extras.append(value)

    rows_grad = rows_product(
        [own_scores, scores0, scores1] + extra_scores,
        [student_head, mine0, theirs0, mine1, theirs1] + extras,
        depth,
        [last],
    )
    head_grad = head_total(at, own_part, [back0, back1], extra_parts)
    return (head_grad, rows_grad, loss[:, 0])


def solution(mesh):
    placed = (
        P(("grp", "seq"), None),
        P(("grp", "seq"), None),
        P("seq", None),
        P("seq", None),
        P(("grp", "seq")),
        P(("grp", "seq")),
        P(("grp", "seq")),
    )
    return jax.shard_map(
        body,
        mesh=mesh,
        in_specs=placed,
        out_specs=(P(("grp", "seq"), None), P(("grp", "seq"), None), P(("grp", "seq"))),
        check_vma=False,
    )
```

```python
import jax
import jax.numpy as jnp
from jax import lax
from jax.experimental import pallas as pl
from jax.experimental.pallas import tpu as pltpu
from jax.sharding import PartitionSpec as P

hard_weight = 0.5
CHUNKS = 4
GATE_VMEM = 128 * 1024
MEETING_VMEM = 12 * 1024 * 1024
WIDE_VMEM = 56 * 1024 * 1024
BOTH = ("grp", "seq")


def permuted(value, move):
    groups, count = lax.axis_size("grp"), lax.axis_size("seq")
    pairs = []
    for group in range(groups):
        for place in range(count):
            target = move(group, place)
            if target is not None:
                pairs.append((group * count + place, target[0] * count + target[1] % count))
    return lax.ppermute(value, BOTH, pairs)


def next_chip(group, place):
    return group, place + 2


def previous_chip(group, place):
    return group, place - 2


def other_plane(group, place):
    return 1 - group, place


def other_core(group, place):
    return group, place + 1 - 2 * (place % 2)


def extra_early(group, place):
    if place % 2 == 0:
        return group, place + 1
    return (group, place + 3) if place // 2 % 2 == 0 else None


def extra_late(group, place):
    return (group, place + 3) if place % 2 == 1 and place // 2 % 2 == 1 else None


def extra_back(group, place):
    return group, place - 3 + 2 * (place % 2)


def gate(values, ready, flops=0):
    operands = list(values) + list(ready)
    anywhere = pl.BlockSpec(memory_space=pl.ANY)
    return pl.pallas_call(
        lambda *refs: None,
        out_shape=[jax.ShapeDtypeStruct(value.shape, value.dtype) for value in values],
        in_specs=[anywhere] * len(operands),
        out_specs=[anywhere] * len(values),
        input_output_aliases={index: index for index in range(len(values))},
        compiler_params=pltpu.CompilerParams(vmem_limit_bytes=GATE_VMEM),
        cost_estimate=pl.CostEstimate(flops=flops, bytes_accessed=0, transcendentals=0),
    )(*operands)


def packed(at, student_head, teacher_head, places, ready=()):
    depth, depth_t = student_head.shape[1], teacher_head.shape[1]

    def kernel(at_ref, student_ref, teacher_ref, *refs):
        outs, sems = refs[len(ready) : -1], refs[-1]
        copies = []
        for index, (moves, start, rows) in enumerate(places):
            first = pl.multiple_of(at_ref[0] + start, 16) if moves else start
            for half, (source, lo, wide) in enumerate(
                [(student_ref, 0, depth), (teacher_ref, depth, depth_t)]
            ):
                copies.append(
                    pltpu.make_async_copy(
                        source.at[pl.ds(first, rows), :],
                        outs[index].at[:, pl.ds(lo, wide)],
                        sems.at[2 * index + half],
                    )
                )
        for copy in copies:
            copy.start()
        for copy in copies:
            copy.wait()

    anywhere = pl.BlockSpec(memory_space=pl.ANY)
    return pl.pallas_call(
        kernel,
        out_shape=[
            jax.ShapeDtypeStruct((rows, depth + depth_t), student_head.dtype) for _, _, rows in places
        ],
        in_specs=[pl.BlockSpec(memory_space=pltpu.SMEM)]
        + [pl.BlockSpec(memory_space=pltpu.HBM)] * 2
        + [anywhere] * len(ready),
        out_specs=[anywhere] * len(places),
        scratch_shapes=[pltpu.SemaphoreType.DMA((2 * len(places),))],
        compiler_params=pltpu.CompilerParams(vmem_limit_bytes=WIDE_VMEM),
    )(at, student_head, teacher_head, *ready)


def head_total(at, own_part, backs, extras):
    width, depth = own_part.shape
    half = width // 2
    quarter = half // 2
    whole = pl.BlockSpec(memory_space=pltpu.VMEM)

    def kernel(at_ref, own_ref, back0, back1, extra0, extra1, out_ref, sum_ref, sems):
        low = at_ref[0] == 0
        copies = []
        for stage, back in enumerate((back0, back1)):
            for side in range(2):
                base = at_ref[0] if side == 0 else half - at_ref[0]
                rows = pl.ds(pl.multiple_of(base + stage * quarter, quarter), quarter)
                picked = pl.ds(stage * quarter, quarter)
                first = low if side == 0 else jnp.logical_not(low)
                extra = jnp.where(first, extra0[picked, :], extra1[picked, :])
                sum_ref[rows, :] = (
                    own_ref[rows, :]
                    + back[pl.ds(side * quarter, quarter), :].astype(jnp.float32)
                    + extra.astype(jnp.float32)
                ).astype(sum_ref.dtype)
                copies.append(
                    pltpu.make_async_copy(
                        sum_ref.at[rows, :], out_ref.at[rows, :], sems.at[2 * stage + side]
                    )
                )
                copies[-1].start()
        for copy in copies:
            copy.wait()

    return pl.pallas_call(
        kernel,
        out_shape=jax.ShapeDtypeStruct((width, depth), jnp.bfloat16),
        in_specs=[pl.BlockSpec(memory_space=pltpu.SMEM)] + [whole] * 5,
        out_specs=pl.BlockSpec(memory_space=pl.ANY),
        scratch_shapes=[pltpu.VMEM((width, depth), jnp.bfloat16), pltpu.SemaphoreType.DMA((4,))],
        compiler_params=pltpu.CompilerParams(vmem_limit_bytes=6 * 1024 * 1024),
    )(at, own_part, *backs, *extras)


def pause(order, ready):
    return gate([order], ready, 30_000_000_000)[0]


def free():
    return pl.CostEstimate(flops=0, bytes_accessed=0, transcendentals=0)


def meeting(rows_s, rows_t, panels, panels_t, norm, norm_t, targets, ids, loss, kinds, ready=(), flag=None):
    count, depth = rows_s.shape
    depth_t = rows_t.shape[1]
    start = 0
    if flag is not None:
        panels, start = panels[:2], panels[2]
        panels_t = []
    pieces = len(panels)
    pieces_t = len(panels_t)
    width = panels[0].shape[0] if flag is not None else sum(panel.shape[0] for panel in panels)
    block = count // 2
    part_rows = width // len(kinds)
    whole = pl.BlockSpec(memory_space=pltpu.VMEM)
    contract = (((1,), (1,)), ((), ()))
    flags = [] if flag is None else [flag]

    def kernel(*refs):
        s_ref, t_ref, norm_ref, norm_t_ref, target_ref, ids_ref, loss_in = refs[:7]
        panel_refs = refs[7 : 7 + pieces]
        panel_t_refs = refs[7 + pieces : 7 + pieces + pieces_t]
        flag_refs = refs[7 + pieces + pieces_t :][: len(flags)]
        outs = refs[7 + pieces + pieces_t + len(flags) + len(ready) :]
        score_ref, loss_ref = outs[:2]
        part_refs = outs[2 : 2 + len(kinds)]
        if flags:
            chosen = jnp.where(
                flag_refs[0][0] == 1, panel_refs[0][...], panel_refs[1][pl.ds(start, width), :]
            )
            panel, panel_t = chosen[:, :depth], chosen[:, depth:]
            outs[-1][...] = panel
        else:
            panel = jnp.concatenate([ref[:, :depth] for ref in panel_refs], axis=0)
            panel_t = jnp.concatenate(
                [ref[:, ref.shape[1] - depth_t :] for ref in panel_t_refs], axis=0
            )

        for step in range(2):
            rows = pl.ds(step * block, block)
            zs = lax.dot_general(s_ref[rows, :], panel, contract, preferred_element_type=jnp.float32)
            zt = lax.dot_general(t_ref[rows, :], panel_t, contract, preferred_element_type=jnp.float32)
            ls = zs - norm_ref[rows, :]
            lt = zt - norm_t_ref[rows, :]
            ps = jnp.exp(ls)
            pt = jnp.exp(lt)
            onehot = (target_ref[rows, :] == ids_ref[...]).astype(jnp.float32)
            scores = ((1.0 + hard_weight) * ps - pt - hard_weight * onehot).astype(jnp.bfloat16)
            score_ref[rows, :] = scores
            terms = pt * (lt - ls) - hard_weight * onehot * ls
            loss_ref[:, rows] = loss_in[:, rows] + lax.dot_general(
                jnp.ones((8, width), jnp.float32),
                terms,
                contract,
                precision=lax.Precision.HIGHEST,
                preferred_element_type=jnp.float32,
            )

        part = lax.dot_general(
            score_ref[...], s_ref[...], (((0,), (0,)), ((), ())), preferred_element_type=jnp.float32
        )
        for index, part_ref in enumerate(part_refs):
            part_ref[...] = part[index * part_rows : (index + 1) * part_rows].astype(part_ref.dtype)

    out_shape = [
        jax.ShapeDtypeStruct((count, width), jnp.bfloat16),
        jax.ShapeDtypeStruct((8, count), jnp.float32),
    ] + [jax.ShapeDtypeStruct((part_rows, depth), kind) for kind in kinds]
    if flags:
        out_shape.append(jax.ShapeDtypeStruct((width, depth), jnp.bfloat16))
    return pl.pallas_call(
        kernel,
        out_shape=out_shape,
        in_specs=[whole] * (7 + pieces + pieces_t)
        + [pl.BlockSpec(memory_space=pltpu.SMEM)] * len(flags)
        + [pl.BlockSpec(memory_space=pl.ANY)] * len(ready),
        out_specs=[whole] * len(out_shape),
        compiler_params=pltpu.CompilerParams(vmem_limit_bytes=MEETING_VMEM),
        cost_estimate=free(),
    )(rows_s, rows_t, norm, norm_t, targets, ids, loss, *panels, *panels_t, *flags, *ready)


def rows_product(scores, panels, depth, ready):
    count = scores[0].shape[0]
    block = depth // 7
    inner = sum(panel.shape[0] for panel in panels)

    def kernel(*refs):
        score_refs = refs[: len(scores)]
        panel_refs = refs[len(scores) : len(scores) + len(panels)]
        out_ref, left_ref = refs[-2:]

        @pl.when(pl.program_id(0) == 0)
        def _():
            left_ref[...] = jnp.concatenate([ref[...] for ref in score_refs], axis=1)

        right = jnp.concatenate([ref[...] for ref in panel_refs], axis=0)
        out_ref[...] = jnp.dot(
            left_ref[...], right, preferred_element_type=jnp.float32
        ).astype(out_ref.dtype)

    return pl.pallas_call(
        kernel,
        grid=(7,),
        out_shape=jax.ShapeDtypeStruct((count, depth), jnp.bfloat16),
        in_specs=[pl.BlockSpec((count, score.shape[1]), lambda index: (0, 0)) for score in scores]
        + [pl.BlockSpec((panel.shape[0], block), lambda index: (0, index)) for panel in panels]
        + [pl.BlockSpec(memory_space=pl.ANY)] * len(ready),
        out_specs=pl.BlockSpec((count, block), lambda index: (0, index)),
        scratch_shapes=[pltpu.VMEM((count, inner), jnp.bfloat16)],
        compiler_params=pltpu.CompilerParams(vmem_limit_bytes=WIDE_VMEM),
        cost_estimate=pl.CostEstimate(flops=30_000_000_000, bytes_accessed=0, transcendentals=0),
    )(*scores, *panels, *ready)


def body(student_rows, teacher_rows, student_head, teacher_head, student_lse, teacher_lse, targets):
    count = lax.axis_size("seq")
    place = lax.axis_index("seq")
    plane = lax.axis_index("grp")
    core = place % 2
    width, depth = student_head.shape
    half = width // 2
    piece = half // CHUNKS
    norm = student_lse.astype(jnp.float32)[:, None]
    norm_t = teacher_lse.astype(jnp.float32)[:, None]
    wanted = targets[:, None]
    order = jnp.zeros((8, 128), jnp.float32)
    ids_in = jnp.arange(width, dtype=jnp.int32)
    near = (place - 2) % count
    far = (place - 1 - 2 * core) % count
    extra_id = jnp.where(core == 1, place - 1, place - 3) % count
    from_late = jnp.reshape(jnp.logical_and(core == 0, place // 2 % 2 == 1), (1,)).astype(jnp.int32)

    def stage_ids(stage):
        rows = jnp.arange(half // 2, dtype=jnp.int32) + stage * (half // 2)
        inside = jnp.concatenate([plane * half + rows, (1 - plane) * half + rows])
        return jnp.concatenate([near * width + inside, far * width + inside])

    def meet(panels, panels_t, ids, loss, kinds, ready, flag=None):
        return meeting(
            student_rows, teacher_rows, panels, panels_t, norm, norm_t, wanted, ids[None, :], loss, kinds, ready, flag
        )

    at = jnp.reshape(plane * half, (1,)).astype(jnp.int32)
    chunks = packed(at, student_head, teacher_head, [(True, k * piece, piece) for k in range(2)])
    chunks = list(chunks)
    chunks += packed(
        at,
        student_head,
        teacher_head,
        [(True, k * piece, piece) for k in range(2, 4)] + [(False, 0, width)],
    )
    send = chunks.pop()

    crossed = [permuted(chunks[0], next_chip), permuted(chunks[1], next_chip), None, None]
    early = permuted(send, extra_early)
    swapped = [None] * 4
    own_scores, loss, own_part = meet(
        [student_head],
        [teacher_head],
        place * width + ids_in,
        jnp.zeros((8, student_rows.shape[0]), jnp.float32),
        [jnp.float32],
        [chunks[2]],
    )
    order = pause(order, [own_scores])
    crossed[0], chunks[2], order = gate([crossed[0], chunks[2], order], [])
    swapped[0] = permuted(crossed[0], other_plane)
    crossed[2] = permuted(chunks[2], next_chip)
    order = pause(order, [chunks[2]])
    crossed[1], chunks[3], order = gate([crossed[1], chunks[3], order], [])
    swapped[1] = permuted(crossed[1], other_plane)
    crossed[3] = permuted(chunks[3], next_chip)
    order = pause(order, [chunks[3]])
    crossed[2], order = gate([crossed[2], order], [])
    swapped[2] = permuted(crossed[2], other_plane)
    send, = packed(at, student_head, teacher_head, [(False, 0, half)], [order])
    late = [permuted(send, extra_late), None]
    order = pause(order, [])
    swapped[0], swapped[1], order = gate([swapped[0], swapped[1], order], [])
    mine0 = jnp.concatenate([crossed[0], crossed[1], swapped[0], swapped[1]], axis=0)
    theirs0 = permuted(mine0, other_core)
    order = pause(order, [mine0])
    crossed[3], order = gate([crossed[3], order], [])
    swapped[3] = permuted(crossed[3], other_plane)

    order = pause(order, [])
    theirs0, early, order = gate([theirs0, early, order], [])
    pair = [mine0, theirs0]
    scores0, loss, keep, give = meet(pair, pair, stage_ids(0), loss, [jnp.float32, jnp.bfloat16], [order])
    got = permuted(give, other_core)
    order = pause(order, [give])
    got, order = gate([got, order], [])
    total = (keep + got.astype(jnp.float32)).astype(jnp.bfloat16)
    back0 = permuted(total, previous_chip)

    swapped[2], swapped[3], order = gate([swapped[2], swapped[3], order], [total])
    mine1 = jnp.concatenate([crossed[2], crossed[3], swapped[2], swapped[3]], axis=0)
    theirs1 = permuted(mine1, other_core)
    send, = packed(at, student_head, teacher_head, [(False, half, half)], [order])
    late[1] = permuted(send, extra_late)
    order = pause(order, [mine1])
    theirs1, order = gate([theirs1, order], [])
    pair = [mine1, theirs1]
    scores1, loss, keep, give = meet(pair, pair, stage_ids(1), loss, [jnp.float32, jnp.bfloat16], [order])
    got = permuted(give, other_core)
    order = pause(order, [give])
    got, order = gate([got, order], [])
    total = (keep + got.astype(jnp.float32)).astype(jnp.bfloat16)
    back1 = permuted(total, previous_chip)

    extra_parts, extra_scores, extras = [], [], []
    last = total
    for k in range(2):
        order = pause(order, [last])
        late[k], order = gate([late[k], order], [])
        ids = extra_id * width + k * half + ids_in[:half]
        scores, loss, last, value = meet(
            [late[k], early, k * half], None, ids, loss, [jnp.bfloat16], [order], from_late
        )
        extra_parts.append(permuted(last, extra_back))
        extra_scores.append(scores)
        extras.append(value)

    rows_grad = rows_product(
        [own_scores, scores0, scores1] + extra_scores,
        [student_head, mine0, theirs0, mine1, theirs1] + extras,
        depth,
        [last],
    )
    head_grad = head_total(at, own_part, [back0, back1], extra_parts)
    return (head_grad, rows_grad, loss[0])


def solution(mesh):
    placed = (
        P(("grp", "seq"), None),
        P(("grp", "seq"), None),
        P("seq", None),
        P("seq", None),
        P(("grp", "seq")),
        P(("grp", "seq")),
        P(("grp", "seq")),
    )
    return jax.shard_map(
        body,
        mesh=mesh,
        in_specs=placed,
        out_specs=(P(("grp", "seq"), None), P(("grp", "seq"), None), P(("grp", "seq"))),
        check_vma=False,
    )
```

```python
import jax
import jax.numpy as jnp
from jax import lax
from jax.experimental import pallas as pl
from jax.experimental.pallas import tpu as pltpu
from jax.sharding import PartitionSpec as P

hard_weight = 0.5
CHUNKS = 4
GATE_VMEM = 128 * 1024
MEETING_VMEM = 12 * 1024 * 1024
WIDE_VMEM = 56 * 1024 * 1024
BOTH = ("grp", "seq")


def permuted(value, move):
    groups, count = lax.axis_size("grp"), lax.axis_size("seq")
    pairs = []
    for group in range(groups):
        for place in range(count):
            target = move(group, place)
            if target is not None:
                pairs.append((group * count + place, target[0] * count + target[1] % count))
    return lax.ppermute(value, BOTH, pairs)


def next_chip(group, place):
    return group, place + 2


def previous_chip(group, place):
    return group, place - 2


def other_plane(group, place):
    return 1 - group, place


def other_core(group, place):
    return group, place + 1 - 2 * (place % 2)


def extra_early(group, place):
    if place % 2 == 0:
        return group, place + 1
    return (group, place + 3) if place // 2 % 2 == 0 else None


def extra_late(group, place):
    return (group, place + 3) if place % 2 == 1 and place // 2 % 2 == 1 else None


def extra_back(group, place):
    return group, place - 3 + 2 * (place % 2)


def gate(values, ready, flops=0):
    operands = list(values) + list(ready)
    anywhere = pl.BlockSpec(memory_space=pl.ANY)
    return pl.pallas_call(
        lambda *refs: None,
        out_shape=[jax.ShapeDtypeStruct(value.shape, value.dtype) for value in values],
        in_specs=[anywhere] * len(operands),
        out_specs=[anywhere] * len(values),
        input_output_aliases={index: index for index in range(len(values))},
        compiler_params=pltpu.CompilerParams(vmem_limit_bytes=GATE_VMEM),
        cost_estimate=pl.CostEstimate(flops=flops, bytes_accessed=0, transcendentals=0),
    )(*operands)


def packed(at, student_head, teacher_head, places, ready=()):
    depth, depth_t = student_head.shape[1], teacher_head.shape[1]

    def kernel(at_ref, student_ref, teacher_ref, *refs):
        outs, sems = refs[len(ready) : -1], refs[-1]
        copies = []
        for index, (moves, start, rows) in enumerate(places):
            first = pl.multiple_of(at_ref[0] + start, 16) if moves else start
            for half, (source, lo, wide) in enumerate(
                [(student_ref, 0, depth), (teacher_ref, depth, depth_t)]
            ):
                copies.append(
                    pltpu.make_async_copy(
                        source.at[pl.ds(first, rows), :],
                        outs[index].at[:, pl.ds(lo, wide)],
                        sems.at[2 * index + half],
                    )
                )
        for copy in copies:
            copy.start()
        for copy in copies:
            copy.wait()

    anywhere = pl.BlockSpec(memory_space=pl.ANY)
    return pl.pallas_call(
        kernel,
        out_shape=[
            jax.ShapeDtypeStruct((rows, depth + depth_t), student_head.dtype) for _, _, rows in places
        ],
        in_specs=[pl.BlockSpec(memory_space=pltpu.SMEM)]
        + [pl.BlockSpec(memory_space=pltpu.HBM)] * 2
        + [anywhere] * len(ready),
        out_specs=[anywhere] * len(places),
        scratch_shapes=[pltpu.SemaphoreType.DMA((2 * len(places),))],
        compiler_params=pltpu.CompilerParams(vmem_limit_bytes=GATE_VMEM),
    )(at, student_head, teacher_head, *ready)


def head_total(at, own_part, backs, extras):
    width, depth = own_part.shape
    half = width // 2
    quarter = half // 2
    whole = pl.BlockSpec(memory_space=pltpu.VMEM)

    def kernel(at_ref, own_ref, back0, back1, extra0, extra1, out_ref, sum_ref, sems):
        low = at_ref[0] == 0
        copies = []
        for stage, back in enumerate((back0, back1)):
            for side in range(2):
                base = at_ref[0] if side == 0 else half - at_ref[0]
                rows = pl.ds(pl.multiple_of(base + stage * quarter, quarter), quarter)
                picked = pl.ds(stage * quarter, quarter)
                first = low if side == 0 else jnp.logical_not(low)
                extra = jnp.where(first, extra0[picked, :], extra1[picked, :])
                sum_ref[rows, :] = (
                    own_ref[rows, :]
                    + back[pl.ds(side * quarter, quarter), :].astype(jnp.float32)
                    + extra.astype(jnp.float32)
                ).astype(sum_ref.dtype)
                copies.append(
                    pltpu.make_async_copy(
                        sum_ref.at[rows, :], out_ref.at[rows, :], sems.at[2 * stage + side]
                    )
                )
                copies[-1].start()
        for copy in copies:
            copy.wait()

    return pl.pallas_call(
        kernel,
        out_shape=jax.ShapeDtypeStruct((width, depth), jnp.bfloat16),
        in_specs=[pl.BlockSpec(memory_space=pltpu.SMEM)] + [whole] * 5,
        out_specs=pl.BlockSpec(memory_space=pl.ANY),
        scratch_shapes=[pltpu.VMEM((width, depth), jnp.bfloat16), pltpu.SemaphoreType.DMA((4,))],
        compiler_params=pltpu.CompilerParams(vmem_limit_bytes=6 * 1024 * 1024),
    )(at, own_part, *backs, *extras)


def pause(order, ready):
    return gate([order], ready, 30_000_000_000)[0]


def free():
    return pl.CostEstimate(flops=0, bytes_accessed=0, transcendentals=0)


def meeting(rows_s, rows_t, panels, panels_t, norm, norm_t, targets, ids, loss, kinds, ready=(), flag=None):
    count, depth = rows_s.shape
    depth_t = rows_t.shape[1]
    start = 0
    if flag is not None:
        panels, start = panels[:2], panels[2]
        panels_t = []
    pieces = len(panels)
    pieces_t = len(panels_t)
    width = panels[0].shape[0] if flag is not None else sum(panel.shape[0] for panel in panels)
    block = count // 2
    part_rows = width // len(kinds)
    whole = pl.BlockSpec(memory_space=pltpu.VMEM)
    contract = (((1,), (1,)), ((), ()))
    flags = [] if flag is None else [flag]

    def kernel(*refs):
        s_ref, t_ref, norm_ref, norm_t_ref, target_ref, ids_ref, loss_in = refs[:7]
        panel_refs = refs[7 : 7 + pieces]
        panel_t_refs = refs[7 + pieces : 7 + pieces + pieces_t]
        flag_refs = refs[7 + pieces + pieces_t :][: len(flags)]
        outs = refs[7 + pieces + pieces_t + len(flags) + len(ready) :]
        score_ref, loss_ref = outs[:2]
        part_refs = outs[2 : 2 + len(kinds)]
        if flags:
            chosen = jnp.where(
                flag_refs[0][0] == 1, panel_refs[0][...], panel_refs[1][pl.ds(start, width), :]
            )
            panel, panel_t = chosen[:, :depth], chosen[:, depth:]
            outs[-1][...] = panel
        else:
            panel = jnp.concatenate([ref[:, :depth] for ref in panel_refs], axis=0)
            panel_t = jnp.concatenate(
                [ref[:, ref.shape[1] - depth_t :] for ref in panel_t_refs], axis=0
            )

        for step in range(2):
            rows = pl.ds(step * block, block)
            zs = lax.dot_general(s_ref[rows, :], panel, contract, preferred_element_type=jnp.float32)
            zt = lax.dot_general(t_ref[rows, :], panel_t, contract, preferred_element_type=jnp.float32)
            ls = zs - norm_ref[rows, :]
            lt = zt - norm_t_ref[rows, :]
            ps = jnp.exp(ls)
            pt = jnp.exp(lt)
            onehot = (target_ref[rows, :] == ids_ref[...]).astype(jnp.float32)
            scores = ((1.0 + hard_weight) * ps - pt - hard_weight * onehot).astype(jnp.bfloat16)
            score_ref[rows, :] = scores
            terms = pt * (lt - ls) - hard_weight * onehot * ls
            loss_ref[:, rows] = loss_in[:, rows] + lax.dot_general(
                jnp.ones((8, width), jnp.float32),
                terms,
                contract,
                precision=lax.Precision.HIGHEST,
                preferred_element_type=jnp.float32,
            )

        part = lax.dot_general(
            score_ref[...], s_ref[...], (((0,), (0,)), ((), ())), preferred_element_type=jnp.float32
        )
        for index, part_ref in enumerate(part_refs):
            part_ref[...] = part[index * part_rows : (index + 1) * part_rows].astype(part_ref.dtype)

    out_shape = [
        jax.ShapeDtypeStruct((count, width), jnp.bfloat16),
        jax.ShapeDtypeStruct((8, count), jnp.float32),
    ] + [jax.ShapeDtypeStruct((part_rows, depth), kind) for kind in kinds]
    if flags:
        out_shape.append(jax.ShapeDtypeStruct((width, depth), jnp.bfloat16))
    return pl.pallas_call(
        kernel,
        out_shape=out_shape,
        in_specs=[whole] * (7 + pieces + pieces_t)
        + [pl.BlockSpec(memory_space=pltpu.SMEM)] * len(flags)
        + [pl.BlockSpec(memory_space=pl.ANY)] * len(ready),
        out_specs=[whole] * len(out_shape),
        compiler_params=pltpu.CompilerParams(vmem_limit_bytes=MEETING_VMEM),
        cost_estimate=free(),
    )(rows_s, rows_t, norm, norm_t, targets, ids, loss, *panels, *panels_t, *flags, *ready)


def rows_product(scores, panels, depth, ready):
    count = scores[0].shape[0]
    block = depth // 7
    inner = sum(panel.shape[0] for panel in panels)

    def kernel(*refs):
        score_refs = refs[: len(scores)]
        panel_refs = refs[len(scores) : len(scores) + len(panels)]
        out_ref, left_ref = refs[-2:]

        @pl.when(pl.program_id(0) == 0)
        def _():
            left_ref[...] = jnp.concatenate([ref[...] for ref in score_refs], axis=1)

        right = jnp.concatenate([ref[...] for ref in panel_refs], axis=0)
        out_ref[...] = jnp.dot(
            left_ref[...], right, preferred_element_type=jnp.float32
        ).astype(out_ref.dtype)

    return pl.pallas_call(
        kernel,
        grid=(7,),
        out_shape=jax.ShapeDtypeStruct((count, depth), jnp.bfloat16),
        in_specs=[pl.BlockSpec((count, score.shape[1]), lambda index: (0, 0)) for score in scores]
        + [pl.BlockSpec((panel.shape[0], block), lambda index: (0, index)) for panel in panels]
        + [pl.BlockSpec(memory_space=pl.ANY)] * len(ready),
        out_specs=pl.BlockSpec((count, block), lambda index: (0, index)),
        scratch_shapes=[pltpu.VMEM((count, inner), jnp.bfloat16)],
        compiler_params=pltpu.CompilerParams(vmem_limit_bytes=WIDE_VMEM),
        cost_estimate=pl.CostEstimate(flops=30_000_000_000, bytes_accessed=0, transcendentals=0),
    )(*scores, *panels, *ready)


def body(student_rows, teacher_rows, student_head, teacher_head, student_lse, teacher_lse, targets):
    count = lax.axis_size("seq")
    place = lax.axis_index("seq")
    plane = lax.axis_index("grp")
    core = place % 2
    width, depth = student_head.shape
    half = width // 2
    piece = half // CHUNKS
    norm = student_lse.astype(jnp.float32)[:, None]
    norm_t = teacher_lse.astype(jnp.float32)[:, None]
    wanted = targets[:, None]
    order = jnp.zeros((8, 128), jnp.float32)
    ids_in = jnp.arange(width, dtype=jnp.int32)
    near = (place - 2) % count
    far = (place - 1 - 2 * core) % count
    extra_id = jnp.where(core == 1, place - 1, place - 3) % count
    from_late = jnp.reshape(jnp.logical_and(core == 0, place // 2 % 2 == 1), (1,)).astype(jnp.int32)

    def stage_ids(stage):
        rows = jnp.arange(half // 2, dtype=jnp.int32) + stage * (half // 2)
        inside = jnp.concatenate([plane * half + rows, (1 - plane) * half + rows])
        return jnp.concatenate([near * width + inside, far * width + inside])

    def meet(panels, panels_t, ids, loss, kinds, ready, flag=None):
        return meeting(
            student_rows, teacher_rows, panels, panels_t, norm, norm_t, wanted, ids[None, :], loss, kinds, ready, flag
        )

    at = jnp.reshape(plane * half, (1,)).astype(jnp.int32)
    chunks = packed(at, student_head, teacher_head, [(True, k * piece, piece) for k in range(2)])
    chunks = list(chunks)
    chunks += packed(
        at,
        student_head,
        teacher_head,
        [(True, k * piece, piece) for k in range(2, 4)]
        + [(False, 0, width), (False, 0, half), (False, half, half)],
    )
    send, send0, send1 = chunks[4:]
    chunks = chunks[:4]

    crossed = [permuted(chunks[0], next_chip), permuted(chunks[1], next_chip), None, None]
    early = permuted(send, extra_early)
    swapped = [None] * 4
    own_scores, loss, own_part = meet(
        [student_head],
        [teacher_head],
        place * width + ids_in,
        jnp.zeros((8, student_rows.shape[0]), jnp.float32),
        [jnp.float32],
        [chunks[2]],
    )
    order = pause(order, [own_scores])
    crossed[0], chunks[2], order = gate([crossed[0], chunks[2], order], [])
    swapped[0] = permuted(crossed[0], other_plane)
    crossed[2] = permuted(chunks[2], next_chip)
    order = pause(order, [chunks[2]])
    crossed[1], chunks[3], order = gate([crossed[1], chunks[3], order], [])
    swapped[1] = permuted(crossed[1], other_plane)
    crossed[3] = permuted(chunks[3], next_chip)
    order = pause(order, [chunks[3]])
    crossed[2], send0, order = gate([crossed[2], send0, order], [])
    swapped[2] = permuted(crossed[2], other_plane)
    late = [permuted(send0, extra_late), None]
    order = pause(order, [crossed[2], send0])
    swapped[0], swapped[1], order = gate([swapped[0], swapped[1], order], [])
    mine0 = jnp.concatenate([crossed[0], crossed[1], swapped[0], swapped[1]], axis=0)
    theirs0 = permuted(mine0, other_core)
    order = pause(order, [mine0])
    crossed[3], order = gate([crossed[3], order], [])
    swapped[3] = permuted(crossed[3], other_plane)

    order = pause(order, [])
    theirs0, early, order = gate([theirs0, early, order], [])
    pair = [mine0, theirs0]
    scores0, loss, keep, give = meet(pair, pair, stage_ids(0), loss, [jnp.float32, jnp.bfloat16], [order])
    got = permuted(give, other_core)
    order = pause(order, [give])
    got, order = gate([got, order], [])
    total = (keep + got.astype(jnp.float32)).astype(jnp.bfloat16)
    back0 = permuted(total, previous_chip)

    swapped[2], swapped[3], order = gate([swapped[2], swapped[3], order], [total])
    mine1 = jnp.concatenate([crossed[2], crossed[3], swapped[2], swapped[3]], axis=0)
    theirs1 = permuted(mine1, other_core)
    send1, order = gate([send1, order], [])
    late[1] = permuted(send1, extra_late)
    order = pause(order, [mine1])
    theirs1, order = gate([theirs1, order], [])
    pair = [mine1, theirs1]
    scores1, loss, keep, give = meet(pair, pair, stage_ids(1), loss, [jnp.float32, jnp.bfloat16], [order])
    got = permuted(give, other_core)
    order = pause(order, [give])
    got, order = gate([got, order], [])
    total = (keep + got.astype(jnp.float32)).astype(jnp.bfloat16)
    back1 = permuted(total, previous_chip)

    extra_parts, extra_scores, extras = [], [], []
    last = total
    for k in range(2):
        order = pause(order, [last])
        late[k], order = gate([late[k], order], [])
        ids = extra_id * width + k * half + ids_in[:half]
        scores, loss, last, value = meet(
            [late[k], early, k * half], None, ids, loss, [jnp.bfloat16], [order], from_late
        )
        extra_parts.append(permuted(last, extra_back))
        extra_scores.append(scores)
        extras.append(value)

    rows_grad = rows_product(
        [own_scores, scores0, scores1] + extra_scores,
        [student_head, mine0, theirs0, mine1, theirs1] + extras,
        depth,
        [last],
    )
    head_grad = head_total(at, own_part, [back0, back1], extra_parts)
    return (head_grad, rows_grad, loss[0])


def solution(mesh):
    placed = (
        P(("grp", "seq"), None),
        P(("grp", "seq"), None),
        P("seq", None),
        P("seq", None),
        P(("grp", "seq")),
        P(("grp", "seq")),
        P(("grp", "seq")),
    )
    return jax.shard_map(
        body,
        mesh=mesh,
        in_specs=placed,
        out_specs=(P(("grp", "seq"), None), P(("grp", "seq"), None), P(("grp", "seq"))),
        check_vma=False,
    )
```

```python
import jax
import jax.numpy as jnp
from jax import lax
from jax.experimental import pallas as pl
from jax.experimental.pallas import tpu as pltpu
from jax.sharding import PartitionSpec as P

hard_weight = 0.5
CHUNKS = 4
GATE_VMEM = 128 * 1024
MEETING_VMEM = 12 * 1024 * 1024
WIDE_VMEM = 56 * 1024 * 1024
BOTH = ("grp", "seq")


def permuted(value, move):
    groups, count = lax.axis_size("grp"), lax.axis_size("seq")
    pairs = []
    for group in range(groups):
        for place in range(count):
            target = move(group, place)
            if target is not None:
                pairs.append((group * count + place, target[0] * count + target[1] % count))
    return lax.ppermute(value, BOTH, pairs)


def next_chip(group, place):
    return group, place + 2


def previous_chip(group, place):
    return group, place - 2


def other_plane(group, place):
    return 1 - group, place


def other_core(group, place):
    return group, place + 1 - 2 * (place % 2)


def extra_early(group, place):
    if place % 2 == 0:
        return group, place + 1
    return (group, place + 3) if place // 2 % 2 == 0 else None


def extra_late(group, place):
    return (group, place + 3) if place % 2 == 1 and place // 2 % 2 == 1 else None


def extra_back(group, place):
    return group, place - 3 + 2 * (place % 2)


def gate(values, ready, flops=0):
    operands = list(values) + list(ready)
    anywhere = pl.BlockSpec(memory_space=pl.ANY)
    return pl.pallas_call(
        lambda *refs: None,
        out_shape=[jax.ShapeDtypeStruct(value.shape, value.dtype) for value in values],
        in_specs=[anywhere] * len(operands),
        out_specs=[anywhere] * len(values),
        input_output_aliases={index: index for index in range(len(values))},
        compiler_params=pltpu.CompilerParams(vmem_limit_bytes=GATE_VMEM),
        cost_estimate=pl.CostEstimate(flops=flops, bytes_accessed=0, transcendentals=0),
    )(*operands)


def packed(at, student_head, teacher_head, places, ready=()):
    depth, depth_t = student_head.shape[1], teacher_head.shape[1]

    def kernel(at_ref, student_ref, teacher_ref, *refs):
        outs, sems = refs[len(ready) : -1], refs[-1]
        copies = []
        for index, (moves, start, rows) in enumerate(places):
            first = pl.multiple_of(at_ref[0] + start, 16) if moves else start
            for half, (source, lo, wide) in enumerate(
                [(student_ref, 0, depth), (teacher_ref, depth, depth_t)]
            ):
                copies.append(
                    pltpu.make_async_copy(
                        source.at[pl.ds(first, rows), :],
                        outs[index].at[:, pl.ds(lo, wide)],
                        sems.at[2 * index + half],
                    )
                )
        for copy in copies:
            copy.start()
        for copy in copies:
            copy.wait()

    anywhere = pl.BlockSpec(memory_space=pl.ANY)
    return pl.pallas_call(
        kernel,
        out_shape=[
            jax.ShapeDtypeStruct((rows, depth + depth_t), student_head.dtype) for _, _, rows in places
        ],
        in_specs=[pl.BlockSpec(memory_space=pltpu.SMEM)]
        + [pl.BlockSpec(memory_space=pltpu.HBM)] * 2
        + [anywhere] * len(ready),
        out_specs=[anywhere] * len(places),
        scratch_shapes=[pltpu.SemaphoreType.DMA((2 * len(places),))],
        compiler_params=pltpu.CompilerParams(vmem_limit_bytes=GATE_VMEM),
    )(at, student_head, teacher_head, *ready)


def head_total(at, own_part, backs, extras):
    width, depth = own_part.shape
    half = width // 2
    quarter = half // 2
    whole = pl.BlockSpec(memory_space=pltpu.VMEM)

    def kernel(at_ref, own_ref, back0, back1, extra0, extra1, out_ref, sum_ref, sems):
        low = at_ref[0] == 0
        copies = []
        for stage, back in enumerate((back0, back1)):
            for side in range(2):
                base = at_ref[0] if side == 0 else half - at_ref[0]
                rows = pl.ds(pl.multiple_of(base + stage * quarter, quarter), quarter)
                picked = pl.ds(stage * quarter, quarter)
                first = low if side == 0 else jnp.logical_not(low)
                extra = jnp.where(first, extra0[picked, :], extra1[picked, :])
                sum_ref[rows, :] = (
                    own_ref[rows, :]
                    + back[pl.ds(side * quarter, quarter), :].astype(jnp.float32)
                    + extra.astype(jnp.float32)
                ).astype(sum_ref.dtype)
                copies.append(
                    pltpu.make_async_copy(
                        sum_ref.at[rows, :], out_ref.at[rows, :], sems.at[2 * stage + side]
                    )
                )
                copies[-1].start()
        for copy in copies:
            copy.wait()

    return pl.pallas_call(
        kernel,
        out_shape=jax.ShapeDtypeStruct((width, depth), jnp.bfloat16),
        in_specs=[pl.BlockSpec(memory_space=pltpu.SMEM)] + [whole] * 5,
        out_specs=pl.BlockSpec(memory_space=pl.ANY),
        scratch_shapes=[pltpu.VMEM((width, depth), jnp.bfloat16), pltpu.SemaphoreType.DMA((4,))],
        compiler_params=pltpu.CompilerParams(vmem_limit_bytes=6 * 1024 * 1024),
    )(at, own_part, *backs, *extras)


def pause(order, ready):
    return gate([order], ready, 30_000_000_000)[0]


def free():
    return pl.CostEstimate(flops=0, bytes_accessed=0, transcendentals=0)


def meeting(rows_s, rows_t, panels, panels_t, norm, norm_t, targets, ids, loss, kinds, ready=(), flag=None):
    count, depth = rows_s.shape
    depth_t = rows_t.shape[1]
    start = 0
    if flag is not None:
        panels, start = panels[:2], panels[2]
        panels_t = []
    pieces = len(panels)
    pieces_t = len(panels_t)
    width = panels[0].shape[0] if flag is not None else sum(panel.shape[0] for panel in panels)
    block = count // 2
    part_rows = width // len(kinds)
    whole = pl.BlockSpec(memory_space=pltpu.VMEM)
    contract = (((1,), (1,)), ((), ()))
    flags = [] if flag is None else [flag]

    def kernel(*refs):
        s_ref, t_ref, norm_ref, norm_t_ref, target_ref, ids_ref, loss_in = refs[:7]
        panel_refs = refs[7 : 7 + pieces]
        panel_t_refs = refs[7 + pieces : 7 + pieces + pieces_t]
        flag_refs = refs[7 + pieces + pieces_t :][: len(flags)]
        outs = refs[7 + pieces + pieces_t + len(flags) + len(ready) :]
        score_ref, loss_ref = outs[:2]
        part_refs = outs[2 : 2 + len(kinds)]
        if flags:
            chosen = outs[-1]

            @pl.when(flag_refs[0][0] == 1)
            def _():
                chosen[...] = panel_refs[0][...]

            @pl.when(flag_refs[0][0] != 1)
            def _():
                chosen[...] = panel_refs[1][pl.ds(start, width), :]

            panel, panel_t = chosen[:, :depth], chosen[:, depth:]
        else:
            panel = jnp.concatenate([ref[:, :depth] for ref in panel_refs], axis=0)
            panel_t = jnp.concatenate(
                [ref[:, ref.shape[1] - depth_t :] for ref in panel_t_refs], axis=0
            )

        for step in range(2):
            rows = pl.ds(step * block, block)
            zs = lax.dot_general(s_ref[rows, :], panel, contract, preferred_element_type=jnp.float32)
            zt = lax.dot_general(t_ref[rows, :], panel_t, contract, preferred_element_type=jnp.float32)
            ls = zs - norm_ref[rows, :]
            lt = zt - norm_t_ref[rows, :]
            ps = jnp.exp(ls)
            pt = jnp.exp(lt)
            onehot = (target_ref[rows, :] == ids_ref[...]).astype(jnp.float32)
            scores = ((1.0 + hard_weight) * ps - pt - hard_weight * onehot).astype(jnp.bfloat16)
            score_ref[rows, :] = scores
            terms = pt * (lt - ls) - hard_weight * onehot * ls
            loss_ref[:, rows] = loss_in[:, rows] + lax.dot_general(
                jnp.ones((8, width), jnp.float32),
                terms,
                contract,
                precision=lax.Precision.HIGHEST,
                preferred_element_type=jnp.float32,
            )

        part = lax.dot_general(
            score_ref[...], s_ref[...], (((0,), (0,)), ((), ())), preferred_element_type=jnp.float32
        )
        for index, part_ref in enumerate(part_refs):
            part_ref[...] = part[index * part_rows : (index + 1) * part_rows].astype(part_ref.dtype)

    out_shape = [
        jax.ShapeDtypeStruct((count, width), jnp.bfloat16),
        jax.ShapeDtypeStruct((8, count), jnp.float32),
    ] + [jax.ShapeDtypeStruct((part_rows, depth), kind) for kind in kinds]
    if flags:
        out_shape.append(jax.ShapeDtypeStruct((width, depth + depth_t), jnp.bfloat16))
    return pl.pallas_call(
        kernel,
        out_shape=out_shape,
        in_specs=[whole] * (7 + pieces + pieces_t)
        + [pl.BlockSpec(memory_space=pltpu.SMEM)] * len(flags)
        + [pl.BlockSpec(memory_space=pl.ANY)] * len(ready),
        out_specs=[whole] * len(out_shape),
        compiler_params=pltpu.CompilerParams(vmem_limit_bytes=MEETING_VMEM),
        cost_estimate=free(),
    )(rows_s, rows_t, norm, norm_t, targets, ids, loss, *panels, *panels_t, *flags, *ready)


def rows_product(scores, panels, depth, ready):
    count = scores[0].shape[0]
    block = depth // 4
    inner = sum(panel.shape[0] for panel in panels)

    def kernel(*refs):
        score_refs = refs[: len(scores)]
        panel_refs = refs[len(scores) : len(scores) + len(panels)]
        out_ref, left_ref = refs[-2:]

        @pl.when(pl.program_id(0) == 0)
        def _():
            left_ref[...] = jnp.concatenate([ref[...] for ref in score_refs], axis=1)

        right = jnp.concatenate([ref[...] for ref in panel_refs], axis=0)
        out_ref[...] = jnp.dot(
            left_ref[...], right, preferred_element_type=jnp.float32
        ).astype(out_ref.dtype)

    return pl.pallas_call(
        kernel,
        grid=(4,),
        out_shape=jax.ShapeDtypeStruct((count, depth), jnp.bfloat16),
        in_specs=[pl.BlockSpec((count, score.shape[1]), lambda index: (0, 0)) for score in scores]
        + [pl.BlockSpec((panel.shape[0], block), lambda index: (0, index)) for panel in panels]
        + [pl.BlockSpec(memory_space=pl.ANY)] * len(ready),
        out_specs=pl.BlockSpec((count, block), lambda index: (0, index)),
        scratch_shapes=[pltpu.VMEM((count, inner), jnp.bfloat16)],
        compiler_params=pltpu.CompilerParams(vmem_limit_bytes=WIDE_VMEM),
        cost_estimate=pl.CostEstimate(flops=30_000_000_000, bytes_accessed=0, transcendentals=0),
    )(*scores, *panels, *ready)


def body(student_rows, teacher_rows, student_head, teacher_head, student_lse, teacher_lse, targets):
    count = lax.axis_size("seq")
    place = lax.axis_index("seq")
    plane = lax.axis_index("grp")
    core = place % 2
    width, depth = student_head.shape
    half = width // 2
    piece = half // CHUNKS
    norm = student_lse.astype(jnp.float32)[:, None]
    norm_t = teacher_lse.astype(jnp.float32)[:, None]
    wanted = targets[:, None]
    order = jnp.zeros((8, 128), jnp.float32)
    ids_in = jnp.arange(width, dtype=jnp.int32)
    near = (place - 2) % count
    far = (place - 1 - 2 * core) % count
    extra_id = jnp.where(core == 1, place - 1, place - 3) % count
    from_late = jnp.reshape(jnp.logical_and(core == 0, place // 2 % 2 == 1), (1,)).astype(jnp.int32)

    def stage_ids(stage):
        rows = jnp.arange(half // 2, dtype=jnp.int32) + stage * (half // 2)
        inside = jnp.concatenate([plane * half + rows, (1 - plane) * half + rows])
        return jnp.concatenate([near * width + inside, far * width + inside])

    def meet(panels, panels_t, ids, loss, kinds, ready, flag=None):
        return meeting(
            student_rows, teacher_rows, panels, panels_t, norm, norm_t, wanted, ids[None, :], loss, kinds, ready, flag
        )

    at = jnp.reshape(plane * half, (1,)).astype(jnp.int32)
    chunks = packed(at, student_head, teacher_head, [(True, k * piece, piece) for k in range(2)])
    chunks = list(chunks)
    chunks += packed(
        at,
        student_head,
        teacher_head,
        [(True, k * piece, piece) for k in range(2, 4)]
        + [(False, 0, width), (False, 0, half), (False, half, half)],
    )
    send, send0, send1 = chunks[4:]
    chunks = chunks[:4]

    crossed = [permuted(chunks[0], next_chip), permuted(chunks[1], next_chip), None, None]
    early = permuted(send, extra_early)
    swapped = [None] * 4
    order = pause(order, [chunks[0]])
    crossed[0], chunks[2], order = gate([crossed[0], chunks[2], order], [])
    swapped[0] = permuted(crossed[0], other_plane)
    crossed[2] = permuted(chunks[2], next_chip)
    order = pause(order, [chunks[2]])
    crossed[1], chunks[3], order = gate([crossed[1], chunks[3], order], [])
    swapped[1] = permuted(crossed[1], other_plane)
    crossed[3] = permuted(chunks[3], next_chip)
    order = pause(order, [chunks[3]])
    crossed[2], send0, order = gate([crossed[2], send0, order], [])
    swapped[2] = permuted(crossed[2], other_plane)
    late = [permuted(send0, extra_late), None]
    own_scores, loss, own_part = meet(
        [student_head],
        [teacher_head],
        place * width + ids_in,
        jnp.zeros((8, student_rows.shape[0]), jnp.float32),
        [jnp.float32],
        [order],
    )
    order = pause(order, [crossed[2], send0, own_scores])
    swapped[0], swapped[1], order = gate([swapped[0], swapped[1], order], [])
    mine0 = jnp.concatenate([crossed[0], crossed[1], swapped[0], swapped[1]], axis=0)
    theirs0 = permuted(mine0, other_core)
    order = pause(order, [mine0])
    crossed[3], order = gate([crossed[3], order], [])
    swapped[3] = permuted(crossed[3], other_plane)

    order = pause(order, [])
    theirs0, early, order = gate([theirs0, early, order], [])
    pair = [mine0, theirs0]
    scores0, loss, keep, give = meet(pair, pair, stage_ids(0), loss, [jnp.float32, jnp.bfloat16], [order])
    got = permuted(give, other_core)
    order = pause(order, [give])
    got, order = gate([got, order], [])
    total = (keep + got.astype(jnp.float32)).astype(jnp.bfloat16)
    back0 = permuted(total, previous_chip)

    swapped[2], swapped[3], order = gate([swapped[2], swapped[3], order], [total])
    mine1 = jnp.concatenate([crossed[2], crossed[3], swapped[2], swapped[3]], axis=0)
    theirs1 = permuted(mine1, other_core)
    send1, order = gate([send1, order], [])
    late[1] = permuted(send1, extra_late)
    order = pause(order, [mine1])
    theirs1, order = gate([theirs1, order], [])
    pair = [mine1, theirs1]
    scores1, loss, keep, give = meet(pair, pair, stage_ids(1), loss, [jnp.float32, jnp.bfloat16], [order])
    got = permuted(give, other_core)
    order = pause(order, [give])
    got, order = gate([got, order], [])
    total = (keep + got.astype(jnp.float32)).astype(jnp.bfloat16)
    back1 = permuted(total, previous_chip)

    extra_parts, extra_scores, extras = [], [], []
    last = total
    for k in range(2):
        order = pause(order, [last])
        late[k], order = gate([late[k], order], [])
        ids = extra_id * width + k * half + ids_in[:half]
        scores, loss, last, value = meet(
            [late[k], early, k * half], None, ids, loss, [jnp.bfloat16], [order], from_late
        )
        extra_parts.append(permuted(last, extra_back))
        extra_scores.append(scores)
        extras.append(value)

    rows_grad = rows_product(
        [own_scores, scores0, scores1] + extra_scores,
        [student_head, mine0, theirs0, mine1, theirs1] + extras,
        depth,
        [last],
    )
    head_grad = head_total(at, own_part, [back0, back1], extra_parts)
    return (head_grad, rows_grad, loss[0])


def solution(mesh):
    placed = (
        P(("grp", "seq"), None),
        P(("grp", "seq"), None),
        P("seq", None),
        P("seq", None),
        P(("grp", "seq")),
        P(("grp", "seq")),
        P(("grp", "seq")),
    )
    return jax.shard_map(
        body,
        mesh=mesh,
        in_specs=placed,
        out_specs=(P(("grp", "seq"), None), P(("grp", "seq"), None), P(("grp", "seq"))),
        check_vma=False,
    )
```

```python
import jax
import jax.numpy as jnp
from jax import lax
from jax.experimental import pallas as pl
from jax.experimental.pallas import tpu as pltpu
from jax.sharding import PartitionSpec as P

hard_weight = 0.5
CHUNKS = 4
GATE_VMEM = 128 * 1024
MEETING_VMEM = 12 * 1024 * 1024
WIDE_VMEM = 56 * 1024 * 1024
BOTH = ("grp", "seq")


def permuted(value, move):
    groups, count = lax.axis_size("grp"), lax.axis_size("seq")
    pairs = []
    for group in range(groups):
        for place in range(count):
            target = move(group, place)
            if target is not None:
                pairs.append((group * count + place, target[0] * count + target[1] % count))
    return lax.ppermute(value, BOTH, pairs)


def next_chip(group, place):
    return group, place + 2


def previous_chip(group, place):
    return group, place - 2


def other_plane(group, place):
    return 1 - group, place


def other_core(group, place):
    return group, place + 1 - 2 * (place % 2)


def extra_early(group, place):
    if place % 2 == 0:
        return group, place + 1
    return (group, place + 3) if place // 2 % 2 == 0 else None


def extra_late(group, place):
    return (group, place + 3) if place % 2 == 1 and place // 2 % 2 == 1 else None


def extra_back(group, place):
    return group, place - 3 + 2 * (place % 2)


def gate(values, ready, flops=0):
    operands = list(values) + list(ready)
    anywhere = pl.BlockSpec(memory_space=pl.ANY)
    return pl.pallas_call(
        lambda *refs: None,
        out_shape=[jax.ShapeDtypeStruct(value.shape, value.dtype) for value in values],
        in_specs=[anywhere] * len(operands),
        out_specs=[anywhere] * len(values),
        input_output_aliases={index: index for index in range(len(values))},
        compiler_params=pltpu.CompilerParams(vmem_limit_bytes=GATE_VMEM),
        cost_estimate=pl.CostEstimate(flops=flops, bytes_accessed=0, transcendentals=0),
    )(*operands)


def packed(at, student_head, teacher_head, places, ready=()):
    depth, depth_t = student_head.shape[1], teacher_head.shape[1]

    def kernel(at_ref, student_ref, teacher_ref, *refs):
        outs, sems = refs[len(ready) : -1], refs[-1]
        copies = []
        for index, (moves, start, rows) in enumerate(places):
            first = pl.multiple_of(at_ref[0] + start, 16) if moves else start
            for half, (source, lo, wide) in enumerate(
                [(student_ref, 0, depth), (teacher_ref, depth, depth_t)]
            ):
                copies.append(
                    pltpu.make_async_copy(
                        source.at[pl.ds(first, rows), :],
                        outs[index].at[:, pl.ds(lo, wide)],
                        sems.at[2 * index + half],
                    )
                )
        for copy in copies:
            copy.start()
        for copy in copies:
            copy.wait()

    anywhere = pl.BlockSpec(memory_space=pl.ANY)
    return pl.pallas_call(
        kernel,
        out_shape=[
            jax.ShapeDtypeStruct((rows, depth + depth_t), student_head.dtype) for _, _, rows in places
        ],
        in_specs=[pl.BlockSpec(memory_space=pltpu.SMEM)]
        + [pl.BlockSpec(memory_space=pltpu.HBM)] * 2
        + [anywhere] * len(ready),
        out_specs=[anywhere] * len(places),
        scratch_shapes=[pltpu.SemaphoreType.DMA((2 * len(places),))],
        compiler_params=pltpu.CompilerParams(vmem_limit_bytes=GATE_VMEM),
    )(at, student_head, teacher_head, *ready)


def head_total(at, own_part, backs, extra):
    width, depth = own_part.shape
    half = width // 2
    quarter = half // 2
    whole = pl.BlockSpec(memory_space=pltpu.VMEM)

    def kernel(at_ref, own_ref, back0, back1, extra_ref, out_ref, sum_ref, sems):
        copies = []
        for stage, back in enumerate((back0, back1)):
            for side in range(2):
                base = at_ref[0] if side == 0 else half - at_ref[0]
                rows = pl.ds(pl.multiple_of(base + stage * quarter, quarter), quarter)
                sum_ref[rows, :] = (
                    own_ref[rows, :]
                    + back[pl.ds(side * quarter, quarter), :].astype(jnp.float32)
                    + extra_ref[rows, :].astype(jnp.float32)
                ).astype(sum_ref.dtype)
                copies.append(
                    pltpu.make_async_copy(
                        sum_ref.at[rows, :], out_ref.at[rows, :], sems.at[2 * stage + side]
                    )
                )
                copies[-1].start()
        for copy in copies:
            copy.wait()

    return pl.pallas_call(
        kernel,
        out_shape=jax.ShapeDtypeStruct((width, depth), jnp.bfloat16),
        in_specs=[pl.BlockSpec(memory_space=pltpu.SMEM)] + [whole] * 4,
        out_specs=pl.BlockSpec(memory_space=pl.ANY),
        scratch_shapes=[pltpu.VMEM((width, depth), jnp.bfloat16), pltpu.SemaphoreType.DMA((4,))],
        compiler_params=pltpu.CompilerParams(vmem_limit_bytes=6 * 1024 * 1024),
    )(at, own_part, *backs, extra)


def pause(order, ready):
    return gate([order], ready, 30_000_000_000)[0]


def free():
    return pl.CostEstimate(flops=0, bytes_accessed=0, transcendentals=0)


def meeting(rows_s, rows_t, panels, panels_t, norm, norm_t, targets, ids, loss, kinds, ready=(), flag=None):
    count, depth = rows_s.shape
    depth_t = rows_t.shape[1]
    start = 0
    if flag is not None:
        panels, start = panels[:2], panels[2]
        panels_t = []
    pieces = len(panels)
    pieces_t = len(panels_t)
    width = panels[0].shape[0] if flag is not None else sum(panel.shape[0] for panel in panels)
    block = count // 2
    part_rows = width // len(kinds)
    whole = pl.BlockSpec(memory_space=pltpu.VMEM)
    contract = (((1,), (1,)), ((), ()))
    flags = [] if flag is None else [flag]

    def kernel(*refs):
        s_ref, t_ref, norm_ref, norm_t_ref, target_ref, ids_ref, loss_in = refs[:7]
        panel_refs = refs[7 : 7 + pieces]
        panel_t_refs = refs[7 + pieces : 7 + pieces + pieces_t]
        flag_refs = refs[7 + pieces + pieces_t :][: len(flags)]
        outs = refs[7 + pieces + pieces_t + len(flags) + len(ready) :]
        score_ref, loss_ref = outs[:2]
        part_refs = outs[2 : 2 + len(kinds)]
        if flags:
            chosen = outs[-1]

            @pl.when(flag_refs[0][0] == 1)
            def _():
                chosen[...] = panel_refs[0][...]

            @pl.when(flag_refs[0][0] != 1)
            def _():
                chosen[...] = panel_refs[1][pl.ds(start, width), :]

            panel, panel_t = chosen[:, :depth], chosen[:, depth:]
        else:
            panel = jnp.concatenate([ref[:, :depth] for ref in panel_refs], axis=0)
            panel_t = jnp.concatenate(
                [ref[:, ref.shape[1] - depth_t :] for ref in panel_t_refs], axis=0
            )

        for step in range(2):
            rows = pl.ds(step * block, block)
            zs = lax.dot_general(s_ref[rows, :], panel, contract, preferred_element_type=jnp.float32)
            zt = lax.dot_general(t_ref[rows, :], panel_t, contract, preferred_element_type=jnp.float32)
            ls = zs - norm_ref[rows, :]
            lt = zt - norm_t_ref[rows, :]
            ps = jnp.exp(ls)
            pt = jnp.exp(lt)
            onehot = (target_ref[rows, :] == ids_ref[...]).astype(jnp.float32)
            scores = ((1.0 + hard_weight) * ps - pt - hard_weight * onehot).astype(jnp.bfloat16)
            score_ref[rows, :] = scores
            terms = pt * (lt - ls) - hard_weight * onehot * ls
            loss_ref[:, rows] = loss_in[:, rows] + lax.dot_general(
                jnp.ones((8, width), jnp.float32),
                terms,
                contract,
                precision=lax.Precision.HIGHEST,
                preferred_element_type=jnp.float32,
            )

        part = lax.dot_general(
            score_ref[...], s_ref[...], (((0,), (0,)), ((), ())), preferred_element_type=jnp.float32
        )
        for index, part_ref in enumerate(part_refs):
            part_ref[...] = part[index * part_rows : (index + 1) * part_rows].astype(part_ref.dtype)

    out_shape = [
        jax.ShapeDtypeStruct((count, width), jnp.bfloat16),
        jax.ShapeDtypeStruct((8, count), jnp.float32),
    ] + [jax.ShapeDtypeStruct((part_rows, depth), kind) for kind in kinds]
    if flags:
        out_shape.append(jax.ShapeDtypeStruct((width, depth + depth_t), jnp.bfloat16))
    return pl.pallas_call(
        kernel,
        out_shape=out_shape,
        in_specs=[whole] * (7 + pieces + pieces_t)
        + [pl.BlockSpec(memory_space=pltpu.SMEM)] * len(flags)
        + [pl.BlockSpec(memory_space=pl.ANY)] * len(ready),
        out_specs=[whole] * len(out_shape),
        compiler_params=pltpu.CompilerParams(vmem_limit_bytes=MEETING_VMEM),
        cost_estimate=free(),
    )(rows_s, rows_t, norm, norm_t, targets, ids, loss, *panels, *panels_t, *flags, *ready)


def rows_product(scores, panels, depth, ready):
    count = scores[0].shape[0]
    block = depth // 4
    inner = sum(panel.shape[0] for panel in panels)

    def kernel(*refs):
        score_refs = refs[: len(scores)]
        panel_refs = refs[len(scores) : len(scores) + len(panels)]
        out_ref, left_ref = refs[-2:]

        @pl.when(pl.program_id(0) == 0)
        def _():
            left_ref[...] = jnp.concatenate([ref[...] for ref in score_refs], axis=1)

        right = jnp.concatenate([ref[...] for ref in panel_refs], axis=0)
        out_ref[...] = jnp.dot(
            left_ref[...], right, preferred_element_type=jnp.float32
        ).astype(out_ref.dtype)

    return pl.pallas_call(
        kernel,
        grid=(4,),
        out_shape=jax.ShapeDtypeStruct((count, depth), jnp.bfloat16),
        in_specs=[pl.BlockSpec((count, score.shape[1]), lambda index: (0, 0)) for score in scores]
        + [pl.BlockSpec((panel.shape[0], block), lambda index: (0, index)) for panel in panels]
        + [pl.BlockSpec(memory_space=pl.ANY)] * len(ready),
        out_specs=pl.BlockSpec((count, block), lambda index: (0, index)),
        scratch_shapes=[pltpu.VMEM((count, inner), jnp.bfloat16)],
        compiler_params=pltpu.CompilerParams(vmem_limit_bytes=WIDE_VMEM),
        cost_estimate=pl.CostEstimate(flops=30_000_000_000, bytes_accessed=0, transcendentals=0),
    )(*scores, *panels, *ready)


def body(student_rows, teacher_rows, student_head, teacher_head, student_lse, teacher_lse, targets):
    count = lax.axis_size("seq")
    place = lax.axis_index("seq")
    plane = lax.axis_index("grp")
    core = place % 2
    width, depth = student_head.shape
    half = width // 2
    piece = half // CHUNKS
    norm = student_lse.astype(jnp.float32)[:, None]
    norm_t = teacher_lse.astype(jnp.float32)[:, None]
    wanted = targets[:, None]
    order = jnp.zeros((8, 128), jnp.float32)
    ids_in = jnp.arange(width, dtype=jnp.int32)
    near = (place - 2) % count
    far = (place - 1 - 2 * core) % count
    extra_id = jnp.where(core == 1, place - 1, place - 3) % count
    from_late = jnp.reshape(jnp.logical_and(core == 0, place // 2 % 2 == 1), (1,)).astype(jnp.int32)

    def stage_ids(stage):
        rows = jnp.arange(half // 2, dtype=jnp.int32) + stage * (half // 2)
        inside = jnp.concatenate([plane * half + rows, (1 - plane) * half + rows])
        return jnp.concatenate([near * width + inside, far * width + inside])

    def meet(panels, panels_t, ids, loss, kinds, ready, flag=None):
        return meeting(
            student_rows, teacher_rows, panels, panels_t, norm, norm_t, wanted, ids[None, :], loss, kinds, ready, flag
        )

    at = jnp.reshape(plane * half, (1,)).astype(jnp.int32)
    chunks = packed(at, student_head, teacher_head, [(True, k * piece, piece) for k in range(2)])
    chunks = list(chunks)
    chunks += packed(
        at,
        student_head,
        teacher_head,
        [(True, k * piece, piece) for k in range(2, 4)]
        + [(False, 0, width)] * 2,
    )
    send, send0 = chunks[4:]
    chunks = chunks[:4]

    crossed = [permuted(chunks[0], next_chip), permuted(chunks[1], next_chip), None, None]
    early = permuted(send, extra_early)
    swapped = [None] * 4
    order = pause(order, [chunks[0]])
    crossed[0], chunks[2], order = gate([crossed[0], chunks[2], order], [])
    swapped[0] = permuted(crossed[0], other_plane)
    crossed[2] = permuted(chunks[2], next_chip)
    order = pause(order, [chunks[2]])
    crossed[1], chunks[3], order = gate([crossed[1], chunks[3], order], [])
    swapped[1] = permuted(crossed[1], other_plane)
    crossed[3] = permuted(chunks[3], next_chip)
    order = pause(order, [chunks[3]])
    crossed[2], send0, order = gate([crossed[2], send0, order], [])
    swapped[2] = permuted(crossed[2], other_plane)
    late = permuted(send0, extra_late)
    own_scores, loss, own_part = meet(
        [student_head],
        [teacher_head],
        place * width + ids_in,
        jnp.zeros((8, student_rows.shape[0]), jnp.float32),
        [jnp.float32],
        [order],
    )
    order = pause(order, [crossed[2], send0, own_scores])
    swapped[0], swapped[1], order = gate([swapped[0], swapped[1], order], [])
    mine0 = jnp.concatenate([crossed[0], crossed[1], swapped[0], swapped[1]], axis=0)
    theirs0 = permuted(mine0, other_core)
    order = pause(order, [mine0])
    crossed[3], order = gate([crossed[3], order], [])
    swapped[3] = permuted(crossed[3], other_plane)

    order = pause(order, [])
    theirs0, early, order = gate([theirs0, early, order], [])
    pair = [mine0, theirs0]
    scores0, loss, keep, give = meet(pair, pair, stage_ids(0), loss, [jnp.float32, jnp.bfloat16], [order])
    got = permuted(give, other_core)
    order = pause(order, [give])
    got, order = gate([got, order], [])
    total = (keep + got.astype(jnp.float32)).astype(jnp.bfloat16)
    back0 = permuted(total, previous_chip)

    swapped[2], swapped[3], order = gate([swapped[2], swapped[3], order], [total])
    mine1 = jnp.concatenate([crossed[2], crossed[3], swapped[2], swapped[3]], axis=0)
    theirs1 = permuted(mine1, other_core)
    order = pause(order, [mine1])
    theirs1, order = gate([theirs1, order], [])
    pair = [mine1, theirs1]
    scores1, loss, keep, give = meet(pair, pair, stage_ids(1), loss, [jnp.float32, jnp.bfloat16], [order])
    got = permuted(give, other_core)
    order = pause(order, [give])
    got, order = gate([got, order], [])
    total = (keep + got.astype(jnp.float32)).astype(jnp.bfloat16)
    back1 = permuted(total, previous_chip)

    order = pause(order, [total])
    late, order = gate([late, order], [])
    extra_scores, loss, extra_part, extra = meet(
        [late, early, 0], None, extra_id * width + ids_in, loss, [jnp.bfloat16], [order], from_late
    )
    extra_part = permuted(extra_part, extra_back)

    rows_grad = rows_product(
        [own_scores, scores0, scores1, extra_scores],
        [student_head, mine0, theirs0, mine1, theirs1, extra],
        depth,
        [extra_scores],
    )
    head_grad = head_total(at, own_part, [back0, back1], extra_part)
    return (head_grad, rows_grad, loss[0])


def solution(mesh):
    placed = (
        P(("grp", "seq"), None),
        P(("grp", "seq"), None),
        P("seq", None),
        P("seq", None),
        P(("grp", "seq")),
        P(("grp", "seq")),
        P(("grp", "seq")),
    )
    return jax.shard_map(
        body,
        mesh=mesh,
        in_specs=placed,
        out_specs=(P(("grp", "seq"), None), P(("grp", "seq"), None), P(("grp", "seq"))),
        check_vma=False,
    )
```

```python
import jax
import jax.numpy as jnp
from jax import lax
from jax.experimental import pallas as pl
from jax.experimental.pallas import tpu as pltpu
from jax.sharding import PartitionSpec as P

hard_weight = 0.5
CHUNKS = 4
GATE_VMEM = 128 * 1024
MEETING_VMEM = 12 * 1024 * 1024
WIDE_VMEM = 56 * 1024 * 1024
BOTH = ("grp", "seq")


def permuted(value, move):
    groups, count = lax.axis_size("grp"), lax.axis_size("seq")
    pairs = []
    for group in range(groups):
        for place in range(count):
            target = move(group, place)
            if target is not None:
                pairs.append((group * count + place, target[0] * count + target[1] % count))
    return lax.ppermute(value, BOTH, pairs)


def next_chip(group, place):
    return group, place + 2


def previous_chip(group, place):
    return group, place - 2


def other_plane(group, place):
    return 1 - group, place


def other_core(group, place):
    return group, place + 1 - 2 * (place % 2)


def extra_early(group, place):
    if place % 2 == 0:
        return group, place + 1
    return (group, place + 3) if place // 2 % 2 == 0 else None


def extra_late(group, place):
    return (group, place + 3) if place % 2 == 1 and place // 2 % 2 == 1 else None


def extra_back(group, place):
    return group, place - 3 + 2 * (place % 2)


def gate(values, ready, flops=0):
    operands = list(values) + list(ready)
    anywhere = pl.BlockSpec(memory_space=pl.ANY)
    return pl.pallas_call(
        lambda *refs: None,
        out_shape=[jax.ShapeDtypeStruct(value.shape, value.dtype) for value in values],
        in_specs=[anywhere] * len(operands),
        out_specs=[anywhere] * len(values),
        input_output_aliases={index: index for index in range(len(values))},
        compiler_params=pltpu.CompilerParams(vmem_limit_bytes=GATE_VMEM),
        cost_estimate=pl.CostEstimate(flops=flops, bytes_accessed=0, transcendentals=0),
    )(*operands)


def packed(at, student_head, teacher_head, places, ready=()):
    depth, depth_t = student_head.shape[1], teacher_head.shape[1]

    def kernel(at_ref, student_ref, teacher_ref, *refs):
        outs, sems = refs[len(ready) : -1], refs[-1]
        copies = []
        for index, (moves, start, rows) in enumerate(places):
            first = pl.multiple_of(at_ref[0] + start, 16) if moves else start
            for half, (source, lo, wide) in enumerate(
                [(student_ref, 0, depth), (teacher_ref, depth, depth_t)]
            ):
                copies.append(
                    pltpu.make_async_copy(
                        source.at[pl.ds(first, rows), :],
                        outs[index].at[:, pl.ds(lo, wide)],
                        sems.at[2 * index + half],
                    )
                )
        for copy in copies:
            copy.start()
        for copy in copies:
            copy.wait()

    anywhere = pl.BlockSpec(memory_space=pl.ANY)
    return pl.pallas_call(
        kernel,
        out_shape=[
            jax.ShapeDtypeStruct((rows, depth + depth_t), student_head.dtype) for _, _, rows in places
        ],
        in_specs=[pl.BlockSpec(memory_space=pltpu.SMEM)]
        + [pl.BlockSpec(memory_space=pltpu.HBM)] * 2
        + [anywhere] * len(ready),
        out_specs=[anywhere] * len(places),
        scratch_shapes=[pltpu.SemaphoreType.DMA((2 * len(places),))],
        compiler_params=pltpu.CompilerParams(vmem_limit_bytes=GATE_VMEM),
    )(at, student_head, teacher_head, *ready)


def head_total(at, own_part, backs, extra):
    width, depth = own_part.shape
    half = width // 2
    quarter = half // 2
    whole = pl.BlockSpec(memory_space=pltpu.VMEM)

    def kernel(at_ref, own_ref, back0, back1, extra_ref, out_ref, sum_ref, sems):
        copies = []
        for stage, back in enumerate((back0, back1)):
            for side in range(2):
                base = at_ref[0] if side == 0 else half - at_ref[0]
                rows = pl.ds(pl.multiple_of(base + stage * quarter, quarter), quarter)
                sum_ref[rows, :] = (
                    own_ref[rows, :]
                    + back[pl.ds(side * quarter, quarter), :].astype(jnp.float32)
                    + extra_ref[rows, :].astype(jnp.float32)
                ).astype(sum_ref.dtype)
                copies.append(
                    pltpu.make_async_copy(
                        sum_ref.at[rows, :], out_ref.at[rows, :], sems.at[2 * stage + side]
                    )
                )
                copies[-1].start()
        for copy in copies:
            copy.wait()

    return pl.pallas_call(
        kernel,
        out_shape=jax.ShapeDtypeStruct((width, depth), jnp.bfloat16),
        in_specs=[pl.BlockSpec(memory_space=pltpu.SMEM)] + [whole] * 4,
        out_specs=pl.BlockSpec(memory_space=pl.ANY),
        scratch_shapes=[pltpu.VMEM((width, depth), jnp.bfloat16), pltpu.SemaphoreType.DMA((4,))],
        compiler_params=pltpu.CompilerParams(vmem_limit_bytes=6 * 1024 * 1024),
    )(at, own_part, *backs, extra)


def pause(order, ready):
    return gate([order], ready, 30_000_000_000)[0]


def free():
    return pl.CostEstimate(flops=0, bytes_accessed=0, transcendentals=0)


def meeting(rows_s, rows_t, panels, panels_t, norm, norm_t, targets, ids, loss, kinds, ready=(), flag=None):
    count, depth = rows_s.shape
    depth_t = rows_t.shape[1]
    start = 0
    if flag is not None:
        panels, start = panels[:2], panels[2]
        panels_t = []
    pieces = len(panels)
    pieces_t = len(panels_t)
    width = panels[0].shape[0] if flag is not None else sum(panel.shape[0] for panel in panels)
    block = count // 2
    part_rows = width // len(kinds)
    whole = pl.BlockSpec(memory_space=pltpu.VMEM)
    contract = (((1,), (1,)), ((), ()))
    flags = [] if flag is None else [flag]

    def kernel(*refs):
        s_ref, t_ref, norm_ref, norm_t_ref, target_ref, ids_ref, loss_in = refs[:7]
        panel_refs = refs[7 : 7 + pieces]
        panel_t_refs = refs[7 + pieces : 7 + pieces + pieces_t]
        flag_refs = refs[7 + pieces + pieces_t :][: len(flags)]
        outs = refs[7 + pieces + pieces_t + len(flags) + len(ready) :]
        score_ref, loss_ref = outs[:2]
        part_refs = outs[2 : 2 + len(kinds)]
        if flags:
            chosen = outs[-1]

            @pl.when(flag_refs[0][0] == 1)
            def _():
                chosen[...] = panel_refs[0][...]

            @pl.when(flag_refs[0][0] != 1)
            def _():
                chosen[...] = panel_refs[1][pl.ds(start, width), :]

            panel, panel_t = chosen[:, :depth], chosen[:, depth:]
        else:
            panel = jnp.concatenate([ref[:, :depth] for ref in panel_refs], axis=0)
            panel_t = jnp.concatenate(
                [ref[:, ref.shape[1] - depth_t :] for ref in panel_t_refs], axis=0
            )

        for step in range(2):
            rows = pl.ds(step * block, block)
            zs = lax.dot_general(s_ref[rows, :], panel, contract, preferred_element_type=jnp.float32)
            zt = lax.dot_general(t_ref[rows, :], panel_t, contract, preferred_element_type=jnp.float32)
            ls = zs - norm_ref[rows, :]
            lt = zt - norm_t_ref[rows, :]
            ps = jnp.exp(ls)
            pt = jnp.exp(lt)
            onehot = (target_ref[rows, :] == ids_ref[...]).astype(jnp.float32)
            scores = ((1.0 + hard_weight) * ps - pt - hard_weight * onehot).astype(jnp.bfloat16)
            score_ref[rows, :] = scores
            terms = pt * (lt - ls) - hard_weight * onehot * ls
            loss_ref[:, rows] = loss_in[:, rows] + lax.dot_general(
                jnp.ones((8, width), jnp.float32),
                terms,
                contract,
                precision=lax.Precision.HIGHEST,
                preferred_element_type=jnp.float32,
            )

        part = lax.dot_general(
            score_ref[...], s_ref[...], (((0,), (0,)), ((), ())), preferred_element_type=jnp.float32
        )
        for index, part_ref in enumerate(part_refs):
            part_ref[...] = part[index * part_rows : (index + 1) * part_rows].astype(part_ref.dtype)

    out_shape = [
        jax.ShapeDtypeStruct((count, width), jnp.bfloat16),
        jax.ShapeDtypeStruct((8, count), jnp.float32),
    ] + [jax.ShapeDtypeStruct((part_rows, depth), kind) for kind in kinds]
    if flags:
        out_shape.append(jax.ShapeDtypeStruct((width, depth + depth_t), jnp.bfloat16))
    return pl.pallas_call(
        kernel,
        out_shape=out_shape,
        in_specs=[whole] * (7 + pieces + pieces_t)
        + [pl.BlockSpec(memory_space=pltpu.SMEM)] * len(flags)
        + [pl.BlockSpec(memory_space=pl.ANY)] * len(ready),
        out_specs=[whole] * len(out_shape),
        compiler_params=pltpu.CompilerParams(vmem_limit_bytes=MEETING_VMEM),
        cost_estimate=free(),
    )(rows_s, rows_t, norm, norm_t, targets, ids, loss, *panels, *panels_t, *flags, *ready)


def rows_product(scores, panels, depth, ready):
    count = scores[0].shape[0]
    block = depth // 4
    inner = sum(panel.shape[0] for panel in panels)

    def kernel(*refs):
        score_refs = refs[: len(scores)]
        panel_refs = refs[len(scores) : len(scores) + len(panels)]
        out_ref, left_ref = refs[-2:]

        @pl.when(pl.program_id(0) == 0)
        def _():
            left_ref[...] = jnp.concatenate([ref[...] for ref in score_refs], axis=1)

        right = jnp.concatenate([ref[...] for ref in panel_refs], axis=0)
        out_ref[...] = jnp.dot(
            left_ref[...], right, preferred_element_type=jnp.float32
        ).astype(out_ref.dtype)

    return pl.pallas_call(
        kernel,
        grid=(4,),
        out_shape=jax.ShapeDtypeStruct((count, depth), jnp.bfloat16),
        in_specs=[pl.BlockSpec((count, score.shape[1]), lambda index: (0, 0)) for score in scores]
        + [pl.BlockSpec((panel.shape[0], block), lambda index: (0, index)) for panel in panels]
        + [pl.BlockSpec(memory_space=pl.ANY)] * len(ready),
        out_specs=pl.BlockSpec((count, block), lambda index: (0, index)),
        scratch_shapes=[pltpu.VMEM((count, inner), jnp.bfloat16)],
        compiler_params=pltpu.CompilerParams(vmem_limit_bytes=WIDE_VMEM),
        cost_estimate=pl.CostEstimate(flops=30_000_000_000, bytes_accessed=0, transcendentals=0),
    )(*scores, *panels, *ready)


def body(student_rows, teacher_rows, student_head, teacher_head, student_lse, teacher_lse, targets):
    count = lax.axis_size("seq")
    place = lax.axis_index("seq")
    plane = lax.axis_index("grp")
    core = place % 2
    width, depth = student_head.shape
    half = width // 2
    piece = half // CHUNKS
    norm = student_lse.astype(jnp.float32)[:, None]
    norm_t = teacher_lse.astype(jnp.float32)[:, None]
    wanted = targets[:, None]
    order = jnp.zeros((8, 128), jnp.float32)
    ids_in = jnp.arange(width, dtype=jnp.int32)
    near = (place - 2) % count
    far = (place - 1 - 2 * core) % count
    extra_id = jnp.where(core == 1, place - 1, place - 3) % count
    from_late = jnp.reshape(jnp.logical_and(core == 0, place // 2 % 2 == 1), (1,)).astype(jnp.int32)

    def stage_ids(stage):
        rows = jnp.arange(half // 2, dtype=jnp.int32) + stage * (half // 2)
        inside = jnp.concatenate([plane * half + rows, (1 - plane) * half + rows])
        return jnp.concatenate([near * width + inside, far * width + inside])

    def meet(panels, panels_t, ids, loss, kinds, ready, flag=None):
        return meeting(
            student_rows, teacher_rows, panels, panels_t, norm, norm_t, wanted, ids[None, :], loss, kinds, ready, flag
        )

    at = jnp.reshape(plane * half, (1,)).astype(jnp.int32)
    chunks = packed(at, student_head, teacher_head, [(True, k * piece, piece) for k in range(2)])
    chunks = list(chunks)
    chunks[0], = gate([chunks[0]], [])
    chunks[1], = gate([chunks[1]], [chunks[0]])
    chunks += packed(
        at,
        student_head,
        teacher_head,
        [(True, k * piece, piece) for k in range(2, 4)]
        + [(False, 0, width)] * 2,
    )
    send, send0 = chunks[4:]
    chunks = chunks[:4]

    crossed = [permuted(chunk, next_chip) for chunk in chunks]
    early = permuted(send, extra_early)
    swapped = [None] * 4
    order = pause(order, [chunks[0]])
    crossed[0], order = gate([crossed[0], order], [])
    swapped[0] = permuted(crossed[0], other_plane)
    order = pause(order, [crossed[0]])
    crossed[1], order = gate([crossed[1], order], [])
    swapped[1] = permuted(crossed[1], other_plane)
    order = pause(order, [crossed[1]])
    crossed[2], send0, order = gate([crossed[2], send0, order], [])
    swapped[2] = permuted(crossed[2], other_plane)
    late = permuted(send0, extra_late)
    own_scores, loss, own_part = meet(
        [student_head],
        [teacher_head],
        place * width + ids_in,
        jnp.zeros((8, student_rows.shape[0]), jnp.float32),
        [jnp.float32],
        [order],
    )
    order = pause(order, [crossed[2], send0, own_scores])
    swapped[0], swapped[1], order = gate([swapped[0], swapped[1], order], [])
    mine0 = jnp.concatenate([crossed[0], crossed[1], swapped[0], swapped[1]], axis=0)
    theirs0 = permuted(mine0, other_core)
    order = pause(order, [mine0])
    crossed[3], order = gate([crossed[3], order], [])
    swapped[3] = permuted(crossed[3], other_plane)

    order = pause(order, [])
    theirs0, early, order = gate([theirs0, early, order], [])
    pair = [mine0, theirs0]
    scores0, loss, keep, give = meet(pair, pair, stage_ids(0), loss, [jnp.float32, jnp.bfloat16], [order])
    got = permuted(give, other_core)
    order = pause(order, [give])
    got, order = gate([got, order], [])
    total = (keep + got.astype(jnp.float32)).astype(jnp.bfloat16)
    back0 = permuted(total, previous_chip)

    swapped[2], swapped[3], order = gate([swapped[2], swapped[3], order], [total])
    mine1 = jnp.concatenate([crossed[2], crossed[3], swapped[2], swapped[3]], axis=0)
    theirs1 = permuted(mine1, other_core)
    order = pause(order, [mine1])
    theirs1, order = gate([theirs1, order], [])
    pair = [mine1, theirs1]
    scores1, loss, keep, give = meet(pair, pair, stage_ids(1), loss, [jnp.float32, jnp.bfloat16], [order])
    got = permuted(give, other_core)
    order = pause(order, [give])
    got, order = gate([got, order], [])
    total = (keep + got.astype(jnp.float32)).astype(jnp.bfloat16)
    back1 = permuted(total, previous_chip)

    order = pause(order, [total])
    late, order = gate([late, order], [])
    extra_scores, loss, extra_part, extra = meet(
        [late, early, 0], None, extra_id * width + ids_in, loss, [jnp.bfloat16], [order], from_late
    )
    extra_part = permuted(extra_part, extra_back)

    rows_grad = rows_product(
        [own_scores, scores0, scores1, extra_scores],
        [student_head, mine0, theirs0, mine1, theirs1, extra],
        depth,
        [extra_scores],
    )
    head_grad = head_total(at, own_part, [back0, back1], extra_part)
    return (head_grad, rows_grad, loss[0])


def solution(mesh):
    placed = (
        P(("grp", "seq"), None),
        P(("grp", "seq"), None),
        P("seq", None),
        P("seq", None),
        P(("grp", "seq")),
        P(("grp", "seq")),
        P(("grp", "seq")),
    )
    return jax.shard_map(
        body,
        mesh=mesh,
        in_specs=placed,
        out_specs=(P(("grp", "seq"), None), P(("grp", "seq"), None), P(("grp", "seq"))),
        check_vma=False,
    )
```

```python
import jax
import jax.numpy as jnp
from jax import lax
from jax.experimental import pallas as pl
from jax.experimental.pallas import tpu as pltpu
from jax.sharding import PartitionSpec as P

hard_weight = 0.5
CHUNKS = 4
GATE_VMEM = 128 * 1024
MEETING_VMEM = 12 * 1024 * 1024
WIDE_VMEM = 56 * 1024 * 1024
BOTH = ("grp", "seq")


def permuted(value, move):
    groups, count = lax.axis_size("grp"), lax.axis_size("seq")
    pairs = []
    for group in range(groups):
        for place in range(count):
            target = move(group, place)
            if target is not None:
                pairs.append((group * count + place, target[0] * count + target[1] % count))
    return lax.ppermute(value, BOTH, pairs)


def next_chip(group, place):
    return group, place + 2


def previous_chip(group, place):
    return group, place - 2


def other_plane(group, place):
    return 1 - group, place


def other_core(group, place):
    return group, place + 1 - 2 * (place % 2)


def extra_early(group, place):
    if place % 2 == 0:
        return group, place + 1
    return (group, place + 3) if place // 2 % 2 == 0 else None


def extra_late(group, place):
    return (group, place + 3) if place % 2 == 1 and place // 2 % 2 == 1 else None


def extra_back(group, place):
    return group, place - 3 + 2 * (place % 2)


def gate(values, ready, flops=0):
    operands = list(values) + list(ready)
    anywhere = pl.BlockSpec(memory_space=pl.ANY)
    return pl.pallas_call(
        lambda *refs: None,
        out_shape=[jax.ShapeDtypeStruct(value.shape, value.dtype) for value in values],
        in_specs=[anywhere] * len(operands),
        out_specs=[anywhere] * len(values),
        input_output_aliases={index: index for index in range(len(values))},
        compiler_params=pltpu.CompilerParams(vmem_limit_bytes=GATE_VMEM),
        cost_estimate=pl.CostEstimate(flops=flops, bytes_accessed=0, transcendentals=0),
    )(*operands)


def packed(at, student_head, teacher_head, places, ready=()):
    depth, depth_t = student_head.shape[1], teacher_head.shape[1]

    def kernel(at_ref, student_ref, teacher_ref, *refs):
        outs, sems = refs[len(ready) : -1], refs[-1]
        copies = []
        for index, (moves, start, rows) in enumerate(places):
            first = pl.multiple_of(at_ref[0] + start, 16) if moves else start
            for half, (source, lo, wide) in enumerate(
                [(student_ref, 0, depth), (teacher_ref, depth, depth_t)]
            ):
                copies.append(
                    pltpu.make_async_copy(
                        source.at[pl.ds(first, rows), :],
                        outs[index].at[:, pl.ds(lo, wide)],
                        sems.at[2 * index + half],
                    )
                )
        for copy in copies:
            copy.start()
        for copy in copies:
            copy.wait()

    anywhere = pl.BlockSpec(memory_space=pl.ANY)
    return pl.pallas_call(
        kernel,
        out_shape=[
            jax.ShapeDtypeStruct((rows, depth + depth_t), student_head.dtype) for _, _, rows in places
        ],
        in_specs=[pl.BlockSpec(memory_space=pltpu.SMEM)]
        + [pl.BlockSpec(memory_space=pltpu.HBM)] * 2
        + [anywhere] * len(ready),
        out_specs=[anywhere] * len(places),
        scratch_shapes=[pltpu.SemaphoreType.DMA((2 * len(places),))],
        compiler_params=pltpu.CompilerParams(vmem_limit_bytes=GATE_VMEM),
    )(at, student_head, teacher_head, *ready)


def head_total(at, own_part, backs, extra):
    width, depth = own_part.shape
    half = width // 2
    quarter = half // 2
    whole = pl.BlockSpec(memory_space=pltpu.VMEM)

    def kernel(at_ref, own_ref, back0, back1, extra_ref, out_ref, sum_ref, sems):
        copies = []
        for stage, back in enumerate((back0, back1)):
            for side in range(2):
                base = at_ref[0] if side == 0 else half - at_ref[0]
                rows = pl.ds(pl.multiple_of(base + stage * quarter, quarter), quarter)
                sum_ref[rows, :] = (
                    own_ref[rows, :]
                    + back[pl.ds(side * quarter, quarter), :].astype(jnp.float32)
                    + extra_ref[rows, :].astype(jnp.float32)
                ).astype(sum_ref.dtype)
                copies.append(
                    pltpu.make_async_copy(
                        sum_ref.at[rows, :], out_ref.at[rows, :], sems.at[2 * stage + side]
                    )
                )
                copies[-1].start()
        for copy in copies:
            copy.wait()

    return pl.pallas_call(
        kernel,
        out_shape=jax.ShapeDtypeStruct((width, depth), jnp.bfloat16),
        in_specs=[pl.BlockSpec(memory_space=pltpu.SMEM)] + [whole] * 4,
        out_specs=pl.BlockSpec(memory_space=pl.ANY),
        scratch_shapes=[pltpu.VMEM((width, depth), jnp.bfloat16), pltpu.SemaphoreType.DMA((4,))],
        compiler_params=pltpu.CompilerParams(vmem_limit_bytes=6 * 1024 * 1024),
    )(at, own_part, *backs, extra)


def pause(order, ready):
    return gate([order], ready, 30_000_000_000)[0]


def free():
    return pl.CostEstimate(flops=0, bytes_accessed=0, transcendentals=0)


def meeting(rows_s, rows_t, panels, panels_t, norm, norm_t, targets, ids, loss, kinds, ready=(), flag=None):
    count, depth = rows_s.shape
    depth_t = rows_t.shape[1]
    start = 0
    if flag is not None:
        panels, start = panels[:2], panels[2]
        panels_t = []
    pieces = len(panels)
    pieces_t = len(panels_t)
    width = panels[0].shape[0] if flag is not None else sum(panel.shape[0] for panel in panels)
    block = count // 2
    part_rows = width // len(kinds)
    whole = pl.BlockSpec(memory_space=pltpu.VMEM)
    contract = (((1,), (1,)), ((), ()))
    flags = [] if flag is None else [flag]

    def kernel(*refs):
        s_ref, t_ref, norm_ref, norm_t_ref, target_ref, ids_ref, loss_in = refs[:7]
        panel_refs = refs[7 : 7 + pieces]
        panel_t_refs = refs[7 + pieces : 7 + pieces + pieces_t]
        flag_refs = refs[7 + pieces + pieces_t :][: len(flags)]
        outs = refs[7 + pieces + pieces_t + len(flags) + len(ready) :]
        score_ref, loss_ref = outs[:2]
        part_refs = outs[2 : 2 + len(kinds)]
        if flags:
            chosen = outs[-1]

            @pl.when(flag_refs[0][0] == 1)
            def _():
                chosen[...] = panel_refs[0][...]

            @pl.when(flag_refs[0][0] != 1)
            def _():
                chosen[...] = panel_refs[1][pl.ds(start, width), :]

            panel, panel_t = chosen[:, :depth], chosen[:, depth:]
        else:
            panel = jnp.concatenate([ref[:, :depth] for ref in panel_refs], axis=0)
            panel_t = jnp.concatenate(
                [ref[:, ref.shape[1] - depth_t :] for ref in panel_t_refs], axis=0
            )

        for step in range(2):
            rows = pl.ds(step * block, block)
            zs = lax.dot_general(s_ref[rows, :], panel, contract, preferred_element_type=jnp.float32)
            zt = lax.dot_general(t_ref[rows, :], panel_t, contract, preferred_element_type=jnp.float32)
            ls = zs - norm_ref[rows, :]
            lt = zt - norm_t_ref[rows, :]
            ps = jnp.exp(ls)
            pt = jnp.exp(lt)
            onehot = (target_ref[rows, :] == ids_ref[...]).astype(jnp.float32)
            scores = ((1.0 + hard_weight) * ps - pt - hard_weight * onehot).astype(jnp.bfloat16)
            score_ref[rows, :] = scores
            terms = pt * (lt - ls) - hard_weight * onehot * ls
            loss_ref[:, rows] = loss_in[:, rows] + lax.dot_general(
                jnp.ones((8, width), jnp.float32),
                terms,
                contract,
                precision=lax.Precision.HIGHEST,
                preferred_element_type=jnp.float32,
            )

        part = lax.dot_general(
            score_ref[...], s_ref[...], (((0,), (0,)), ((), ())), preferred_element_type=jnp.float32
        )
        for index, part_ref in enumerate(part_refs):
            part_ref[...] = part[index * part_rows : (index + 1) * part_rows].astype(part_ref.dtype)

    out_shape = [
        jax.ShapeDtypeStruct((count, width), jnp.bfloat16),
        jax.ShapeDtypeStruct((8, count), jnp.float32),
    ] + [jax.ShapeDtypeStruct((part_rows, depth), kind) for kind in kinds]
    if flags:
        out_shape.append(jax.ShapeDtypeStruct((width, depth + depth_t), jnp.bfloat16))
    return pl.pallas_call(
        kernel,
        out_shape=out_shape,
        in_specs=[whole] * (7 + pieces + pieces_t)
        + [pl.BlockSpec(memory_space=pltpu.SMEM)] * len(flags)
        + [pl.BlockSpec(memory_space=pl.ANY)] * len(ready),
        out_specs=[whole] * len(out_shape),
        compiler_params=pltpu.CompilerParams(vmem_limit_bytes=MEETING_VMEM),
        cost_estimate=free(),
    )(rows_s, rows_t, norm, norm_t, targets, ids, loss, *panels, *panels_t, *flags, *ready)


def rows_product(scores, panels, depth, ready):
    count = scores[0].shape[0]
    block = depth // 4
    inner = sum(panel.shape[0] for panel in panels)

    def kernel(*refs):
        score_refs = refs[: len(scores)]
        panel_refs = refs[len(scores) : len(scores) + len(panels)]
        out_ref, left_ref = refs[-2:]

        @pl.when(pl.program_id(0) == 0)
        def _():
            left_ref[...] = jnp.concatenate([ref[...] for ref in score_refs], axis=1)

        right = jnp.concatenate([ref[...] for ref in panel_refs], axis=0)
        out_ref[...] = jnp.dot(
            left_ref[...], right, preferred_element_type=jnp.float32
        ).astype(out_ref.dtype)

    return pl.pallas_call(
        kernel,
        grid=(4,),
        out_shape=jax.ShapeDtypeStruct((count, depth), jnp.bfloat16),
        in_specs=[pl.BlockSpec((count, score.shape[1]), lambda index: (0, 0)) for score in scores]
        + [pl.BlockSpec((panel.shape[0], block), lambda index: (0, index)) for panel in panels]
        + [pl.BlockSpec(memory_space=pl.ANY)] * len(ready),
        out_specs=pl.BlockSpec((count, block), lambda index: (0, index)),
        scratch_shapes=[pltpu.VMEM((count, inner), jnp.bfloat16)],
        compiler_params=pltpu.CompilerParams(vmem_limit_bytes=WIDE_VMEM),
        cost_estimate=pl.CostEstimate(flops=30_000_000_000, bytes_accessed=0, transcendentals=0),
    )(*scores, *panels, *ready)


def body(student_rows, teacher_rows, student_head, teacher_head, student_lse, teacher_lse, targets):
    count = lax.axis_size("seq")
    place = lax.axis_index("seq")
    plane = lax.axis_index("grp")
    core = place % 2
    width, depth = student_head.shape
    half = width // 2
    piece = half // CHUNKS
    norm = student_lse.astype(jnp.float32)[:, None]
    norm_t = teacher_lse.astype(jnp.float32)[:, None]
    wanted = targets[:, None]
    order = jnp.zeros((8, 128), jnp.float32)
    ids_in = jnp.arange(width, dtype=jnp.int32)
    near = (place - 2) % count
    far = (place - 1 - 2 * core) % count
    extra_id = jnp.where(core == 1, place - 1, place - 3) % count
    from_late = jnp.reshape(jnp.logical_and(core == 0, place // 2 % 2 == 1), (1,)).astype(jnp.int32)

    def stage_ids(stage):
        rows = jnp.arange(half // 2, dtype=jnp.int32) + stage * (half // 2)
        inside = jnp.concatenate([plane * half + rows, (1 - plane) * half + rows])
        return jnp.concatenate([near * width + inside, far * width + inside])

    def meet(panels, panels_t, ids, loss, kinds, ready, flag=None):
        return meeting(
            student_rows, teacher_rows, panels, panels_t, norm, norm_t, wanted, ids[None, :], loss, kinds, ready, flag
        )

    at = jnp.reshape(plane * half, (1,)).astype(jnp.int32)
    chunks = packed(at, student_head, teacher_head, [(True, k * piece, piece) for k in range(2)])
    chunks = list(chunks)
    chunks[0], = gate([chunks[0]], [])
    chunks[1], = gate([chunks[1]], [chunks[0]])
    chunks += packed(
        at,
        student_head,
        teacher_head,
        [(True, k * piece, piece) for k in range(2, 4)]
        + [(False, 0, width)] * 2,
    )
    send, send0 = chunks[4:]
    chunks = chunks[:4]

    crossed = [permuted(chunk, next_chip) for chunk in chunks]
    early = permuted(send, extra_early)
    swapped = [None] * 4
    order = pause(order, [chunks[0]])
    crossed[0], order = gate([crossed[0], order], [])
    swapped[0] = permuted(crossed[0], other_plane)
    order = pause(order, [crossed[0]])
    crossed[1], order = gate([crossed[1], order], [])
    swapped[1] = permuted(crossed[1], other_plane)
    order = pause(order, [crossed[1]])
    crossed[2], send0, order = gate([crossed[2], send0, order], [])
    swapped[2] = permuted(crossed[2], other_plane)
    late = permuted(send0, extra_late)
    order = pause(order, [crossed[2], send0])
    swapped[0], swapped[1], order = gate([swapped[0], swapped[1], order], [])
    mine0 = jnp.concatenate([crossed[0], crossed[1], swapped[0], swapped[1]], axis=0)
    theirs0 = permuted(mine0, other_core)
    order = pause(order, [mine0])
    crossed[3], order = gate([crossed[3], order], [])
    swapped[3] = permuted(crossed[3], other_plane)

    own_scores, loss, own_part = meet(
        [student_head],
        [teacher_head],
        place * width + ids_in,
        jnp.zeros((8, student_rows.shape[0]), jnp.float32),
        [jnp.float32],
        [order],
    )
    order = pause(order, [own_scores])
    theirs0, early, order = gate([theirs0, early, order], [])
    pair = [mine0, theirs0]
    scores0, loss, keep, give = meet(pair, pair, stage_ids(0), loss, [jnp.float32, jnp.bfloat16], [order])
    got = permuted(give, other_core)
    order = pause(order, [give])
    got, order = gate([got, order], [])
    total = (keep + got.astype(jnp.float32)).astype(jnp.bfloat16)
    back0 = permuted(total, previous_chip)

    swapped[2], swapped[3], order = gate([swapped[2], swapped[3], order], [total])
    mine1 = jnp.concatenate([crossed[2], crossed[3], swapped[2], swapped[3]], axis=0)
    theirs1 = permuted(mine1, other_core)
    order = pause(order, [mine1])
    theirs1, order = gate([theirs1, order], [])
    pair = [mine1, theirs1]
    scores1, loss, keep, give = meet(pair, pair, stage_ids(1), loss, [jnp.float32, jnp.bfloat16], [order])
    got = permuted(give, other_core)
    order = pause(order, [give])
    got, order = gate([got, order], [])
    total = (keep + got.astype(jnp.float32)).astype(jnp.bfloat16)
    back1 = permuted(total, previous_chip)

    order = pause(order, [total])
    late, order = gate([late, order], [])
    extra_scores, loss, extra_part, extra = meet(
        [late, early, 0], None, extra_id * width + ids_in, loss, [jnp.bfloat16], [order], from_late
    )
    extra_part, order = gate([extra_part, order], [])
    order = pause(order, [extra_part])
    extra_part = permuted(extra_part, extra_back)

    rows_grad = rows_product(
        [own_scores, scores0, scores1, extra_scores],
        [student_head, mine0, theirs0, mine1, theirs1, extra],
        depth,
        [order],
    )
    head_grad = head_total(at, own_part, [back0, back1], extra_part)
    return (head_grad, rows_grad, loss[0])


def solution(mesh):
    placed = (
        P(("grp", "seq"), None),
        P(("grp", "seq"), None),
        P("seq", None),
        P("seq", None),
        P(("grp", "seq")),
        P(("grp", "seq")),
        P(("grp", "seq")),
    )
    return jax.shard_map(
        body,
        mesh=mesh,
        in_specs=placed,
        out_specs=(P(("grp", "seq"), None), P(("grp", "seq"), None), P(("grp", "seq"))),
        check_vma=False,
    )
```

```python
import jax
import jax.numpy as jnp
from jax import lax
from jax.experimental import pallas as pl
from jax.experimental.pallas import tpu as pltpu
from jax.sharding import PartitionSpec as P

hard_weight = 0.5
CHUNKS = 4
GATE_VMEM = 128 * 1024
MEETING_VMEM = 12 * 1024 * 1024
WIDE_VMEM = 56 * 1024 * 1024
BOTH = ("grp", "seq")


def permuted(value, move):
    groups, count = lax.axis_size("grp"), lax.axis_size("seq")
    pairs = []
    for group in range(groups):
        for place in range(count):
            target = move(group, place)
            if target is not None:
                pairs.append((group * count + place, target[0] * count + target[1] % count))
    return lax.ppermute(value, BOTH, pairs)


def next_chip(group, place):
    return group, place + 2


def previous_chip(group, place):
    return group, place - 2


def other_plane(group, place):
    return 1 - group, place


def other_core(group, place):
    return group, place + 1 - 2 * (place % 2)


def extra_early(group, place):
    if place % 2 == 0:
        return group, place + 1
    return (group, place + 3) if place // 2 % 2 == 0 else None


def extra_late(group, place):
    return (group, place + 3) if place % 2 == 1 and place // 2 % 2 == 1 else None


def extra_back(group, place):
    return group, place - 3 + 2 * (place % 2)


def gate(values, ready, flops=0):
    operands = list(values) + list(ready)
    anywhere = pl.BlockSpec(memory_space=pl.ANY)
    return pl.pallas_call(
        lambda *refs: None,
        out_shape=[jax.ShapeDtypeStruct(value.shape, value.dtype) for value in values],
        in_specs=[anywhere] * len(operands),
        out_specs=[anywhere] * len(values),
        input_output_aliases={index: index for index in range(len(values))},
        compiler_params=pltpu.CompilerParams(vmem_limit_bytes=GATE_VMEM),
        cost_estimate=pl.CostEstimate(flops=flops, bytes_accessed=0, transcendentals=0),
    )(*operands)


def packed(at, student_head, teacher_head, places, ready=()):
    depth, depth_t = student_head.shape[1], teacher_head.shape[1]

    def kernel(at_ref, student_ref, teacher_ref, *refs):
        outs, sems = refs[len(ready) : -1], refs[-1]
        copies = []
        for index, (moves, start, rows) in enumerate(places):
            first = pl.multiple_of(at_ref[0] + start, 16) if moves else start
            for half, (source, lo, wide) in enumerate(
                [(student_ref, 0, depth), (teacher_ref, depth, depth_t)]
            ):
                copies.append(
                    pltpu.make_async_copy(
                        source.at[pl.ds(first, rows), :],
                        outs[index].at[:, pl.ds(lo, wide)],
                        sems.at[2 * index + half],
                    )
                )
        for copy in copies:
            copy.start()
        for copy in copies:
            copy.wait()

    anywhere = pl.BlockSpec(memory_space=pl.ANY)
    return pl.pallas_call(
        kernel,
        out_shape=[
            jax.ShapeDtypeStruct((rows, depth + depth_t), student_head.dtype) for _, _, rows in places
        ],
        in_specs=[pl.BlockSpec(memory_space=pltpu.SMEM)]
        + [pl.BlockSpec(memory_space=pltpu.HBM)] * 2
        + [anywhere] * len(ready),
        out_specs=[anywhere] * len(places),
        scratch_shapes=[pltpu.SemaphoreType.DMA((2 * len(places),))],
        compiler_params=pltpu.CompilerParams(vmem_limit_bytes=GATE_VMEM),
    )(at, student_head, teacher_head, *ready)


def head_total(at, own_part, backs, extra):
    width, depth = own_part.shape
    half = width // 2
    quarter = half // 2
    whole = pl.BlockSpec(memory_space=pltpu.VMEM)

    def kernel(at_ref, own_ref, back0, back1, extra_ref, out_ref, sum_ref, sems):
        copies = []
        for stage, back in enumerate((back0, back1)):
            for side in range(2):
                base = at_ref[0] if side == 0 else half - at_ref[0]
                rows = pl.ds(pl.multiple_of(base + stage * quarter, quarter), quarter)
                sum_ref[rows, :] = (
                    own_ref[rows, :]
                    + back[pl.ds(side * quarter, quarter), :].astype(jnp.float32)
                    + extra_ref[rows, :].astype(jnp.float32)
                ).astype(sum_ref.dtype)
                copies.append(
                    pltpu.make_async_copy(
                        sum_ref.at[rows, :], out_ref.at[rows, :], sems.at[2 * stage + side]
                    )
                )
                copies[-1].start()
        for copy in copies:
            copy.wait()

    return pl.pallas_call(
        kernel,
        out_shape=jax.ShapeDtypeStruct((width, depth), jnp.bfloat16),
        in_specs=[pl.BlockSpec(memory_space=pltpu.SMEM)] + [whole] * 4,
        out_specs=pl.BlockSpec(memory_space=pl.ANY),
        scratch_shapes=[pltpu.VMEM((width, depth), jnp.bfloat16), pltpu.SemaphoreType.DMA((4,))],
        compiler_params=pltpu.CompilerParams(vmem_limit_bytes=6 * 1024 * 1024),
    )(at, own_part, *backs, extra)


def pause(order, ready):
    return gate([order], ready, 30_000_000_000)[0]


def free():
    return pl.CostEstimate(flops=0, bytes_accessed=0, transcendentals=0)


def meeting(rows_s, rows_t, panels, panels_t, norm, norm_t, targets, ids, loss, kinds, ready=(), flag=None):
    count, depth = rows_s.shape
    depth_t = rows_t.shape[1]
    start = 0
    if flag is not None:
        panels, start = panels[:2], panels[2]
        panels_t = []
    pieces = len(panels)
    pieces_t = len(panels_t)
    width = panels[0].shape[0] if flag is not None else sum(panel.shape[0] for panel in panels)
    block = count // 2
    part_rows = width // len(kinds)
    whole = pl.BlockSpec(memory_space=pltpu.VMEM)
    contract = (((1,), (1,)), ((), ()))
    flags = [] if flag is None else [flag]

    def kernel(*refs):
        s_ref, t_ref, norm_ref, norm_t_ref, target_ref, ids_ref, loss_in = refs[:7]
        panel_refs = refs[7 : 7 + pieces]
        panel_t_refs = refs[7 + pieces : 7 + pieces + pieces_t]
        flag_refs = refs[7 + pieces + pieces_t :][: len(flags)]
        outs = refs[7 + pieces + pieces_t + len(flags) + len(ready) :]
        score_ref, loss_ref = outs[:2]
        part_refs = outs[2 : 2 + len(kinds)]
        if flags:
            chosen = outs[-1]

            @pl.when(flag_refs[0][0] == 1)
            def _():
                chosen[...] = panel_refs[0][...]

            @pl.when(flag_refs[0][0] != 1)
            def _():
                chosen[...] = panel_refs[1][pl.ds(start, width), :]

            panel, panel_t = chosen[:, :depth], chosen[:, depth:]
        else:
            panel = jnp.concatenate([ref[:, :depth] for ref in panel_refs], axis=0)
            panel_t = jnp.concatenate(
                [ref[:, ref.shape[1] - depth_t :] for ref in panel_t_refs], axis=0
            )

        for step in range(2):
            rows = pl.ds(step * block, block)
            zs = lax.dot_general(s_ref[rows, :], panel, contract, preferred_element_type=jnp.float32)
            zt = lax.dot_general(t_ref[rows, :], panel_t, contract, preferred_element_type=jnp.float32)
            ls = zs - norm_ref[rows, :]
            lt = zt - norm_t_ref[rows, :]
            ps = jnp.exp(ls)
            pt = jnp.exp(lt)
            onehot = (target_ref[rows, :] == ids_ref[...]).astype(jnp.float32)
            scores = ((1.0 + hard_weight) * ps - pt - hard_weight * onehot).astype(jnp.bfloat16)
            score_ref[rows, :] = scores
            terms = pt * (lt - ls) - hard_weight * onehot * ls
            loss_ref[:, rows] = loss_in[:, rows] + lax.dot_general(
                jnp.ones((8, width), jnp.float32),
                terms,
                contract,
                precision=lax.Precision.HIGHEST,
                preferred_element_type=jnp.float32,
            )

        part = lax.dot_general(
            score_ref[...], s_ref[...], (((0,), (0,)), ((), ())), preferred_element_type=jnp.float32
        )
        for index, part_ref in enumerate(part_refs):
            part_ref[...] = part[index * part_rows : (index + 1) * part_rows].astype(part_ref.dtype)

    out_shape = [
        jax.ShapeDtypeStruct((count, width), jnp.bfloat16),
        jax.ShapeDtypeStruct((8, count), jnp.float32),
    ] + [jax.ShapeDtypeStruct((part_rows, depth), kind) for kind in kinds]
    if flags:
        out_shape.append(jax.ShapeDtypeStruct((width, depth + depth_t), jnp.bfloat16))
    return pl.pallas_call(
        kernel,
        out_shape=out_shape,
        in_specs=[whole] * (7 + pieces + pieces_t)
        + [pl.BlockSpec(memory_space=pltpu.SMEM)] * len(flags)
        + [pl.BlockSpec(memory_space=pl.ANY)] * len(ready),
        out_specs=[whole] * len(out_shape),
        compiler_params=pltpu.CompilerParams(vmem_limit_bytes=MEETING_VMEM),
        cost_estimate=free(),
    )(rows_s, rows_t, norm, norm_t, targets, ids, loss, *panels, *panels_t, *flags, *ready)


def rows_product(scores, panels, depth, ready):
    count = scores[0].shape[0]
    block = depth // 4
    inner = sum(panel.shape[0] for panel in panels)

    def kernel(*refs):
        score_refs = refs[: len(scores)]
        panel_refs = refs[len(scores) : len(scores) + len(panels)]
        out_ref, left_ref = refs[-2:]

        @pl.when(pl.program_id(0) == 0)
        def _():
            left_ref[...] = jnp.concatenate([ref[...] for ref in score_refs], axis=1)

        right = jnp.concatenate([ref[...] for ref in panel_refs], axis=0)
        out_ref[...] = jnp.dot(
            left_ref[...], right, preferred_element_type=jnp.float32
        ).astype(out_ref.dtype)

    return pl.pallas_call(
        kernel,
        grid=(4,),
        out_shape=jax.ShapeDtypeStruct((count, depth), jnp.bfloat16),
        in_specs=[pl.BlockSpec((count, score.shape[1]), lambda index: (0, 0)) for score in scores]
        + [pl.BlockSpec((panel.shape[0], block), lambda index: (0, index)) for panel in panels]
        + [pl.BlockSpec(memory_space=pl.ANY)] * len(ready),
        out_specs=pl.BlockSpec((count, block), lambda index: (0, index)),
        scratch_shapes=[pltpu.VMEM((count, inner), jnp.bfloat16)],
        compiler_params=pltpu.CompilerParams(vmem_limit_bytes=WIDE_VMEM),
        cost_estimate=pl.CostEstimate(flops=30_000_000_000, bytes_accessed=0, transcendentals=0),
    )(*scores, *panels, *ready)


def body(student_rows, teacher_rows, student_head, teacher_head, student_lse, teacher_lse, targets):
    count = lax.axis_size("seq")
    place = lax.axis_index("seq")
    plane = lax.axis_index("grp")
    core = place % 2
    width, depth = student_head.shape
    half = width // 2
    piece = half // CHUNKS
    norm = student_lse.astype(jnp.float32)[:, None]
    norm_t = teacher_lse.astype(jnp.float32)[:, None]
    wanted = targets[:, None]
    order = jnp.zeros((8, 128), jnp.float32)
    ids_in = jnp.arange(width, dtype=jnp.int32)
    near = (place - 2) % count
    far = (place - 1 - 2 * core) % count
    extra_id = jnp.where(core == 1, place - 1, place - 3) % count
    from_late = jnp.reshape(jnp.logical_and(core == 0, place // 2 % 2 == 1), (1,)).astype(jnp.int32)

    def stage_ids(stage):
        rows = jnp.arange(half // 2, dtype=jnp.int32) + stage * (half // 2)
        inside = jnp.concatenate([plane * half + rows, (1 - plane) * half + rows])
        return jnp.concatenate([near * width + inside, far * width + inside])

    def meet(panels, panels_t, ids, loss, kinds, ready, flag=None):
        return meeting(
            student_rows, teacher_rows, panels, panels_t, norm, norm_t, wanted, ids[None, :], loss, kinds, ready, flag
        )

    at = jnp.reshape(plane * half, (1,)).astype(jnp.int32)
    chunks = packed(at, student_head, teacher_head, [(True, k * piece, piece) for k in range(2)])
    chunks = list(chunks)
    chunks[0], = gate([chunks[0]], [])
    chunks[1], = gate([chunks[1]], [chunks[0]])
    chunks += packed(
        at,
        student_head,
        teacher_head,
        [(True, k * piece, piece) for k in range(2, 4)]
        + [(False, 0, width)] * 2,
    )
    send, send0 = chunks[4:]
    chunks = chunks[:4]
    chunks[2], = gate([chunks[2]], [])
    chunks[3], = gate([chunks[3]], [chunks[2]])

    crossed = [permuted(chunk, next_chip) for chunk in chunks]
    early = permuted(send, extra_early)
    swapped = [None] * 4
    order = pause(order, [chunks[0]])
    crossed[0], order = gate([crossed[0], order], [])
    swapped[0] = permuted(crossed[0], other_plane)
    order = pause(order, [crossed[0]])
    crossed[1], order = gate([crossed[1], order], [])
    swapped[1] = permuted(crossed[1], other_plane)
    order = pause(order, [crossed[1]])
    crossed[2], send0, order = gate([crossed[2], send0, order], [])
    swapped[2] = permuted(crossed[2], other_plane)
    late = permuted(send0, extra_late)
    order = pause(order, [crossed[2], send0])
    swapped[0], swapped[1], order = gate([swapped[0], swapped[1], order], [])
    mine0 = jnp.concatenate([crossed[0], crossed[1], swapped[0], swapped[1]], axis=0)
    theirs0 = permuted(mine0, other_core)
    order = pause(order, [mine0])
    crossed[3], order = gate([crossed[3], order], [])
    swapped[3] = permuted(crossed[3], other_plane)

    own_scores, loss, own_part = meet(
        [student_head],
        [teacher_head],
        place * width + ids_in,
        jnp.zeros((8, student_rows.shape[0]), jnp.float32),
        [jnp.float32],
        [order],
    )
    order = pause(order, [own_scores])
    theirs0, early, order = gate([theirs0, early, order], [])
    pair = [mine0, theirs0]
    scores0, loss, keep, give = meet(pair, pair, stage_ids(0), loss, [jnp.float32, jnp.bfloat16], [order])
    got = permuted(give, other_core)
    order = pause(order, [give])
    got, order = gate([got, order], [])
    total = (keep + got.astype(jnp.float32)).astype(jnp.bfloat16)
    back0 = permuted(total, previous_chip)

    swapped[2], swapped[3], order = gate([swapped[2], swapped[3], order], [total])
    mine1 = jnp.concatenate([crossed[2], crossed[3], swapped[2], swapped[3]], axis=0)
    theirs1 = permuted(mine1, other_core)
    order = pause(order, [mine1])
    theirs1, order = gate([theirs1, order], [])
    pair = [mine1, theirs1]
    scores1, loss, keep, give = meet(pair, pair, stage_ids(1), loss, [jnp.float32, jnp.bfloat16], [order])
    got = permuted(give, other_core)
    order = pause(order, [give])
    got, order = gate([got, order], [])
    total = (keep + got.astype(jnp.float32)).astype(jnp.bfloat16)
    back1 = permuted(total, previous_chip)

    order = pause(order, [total])
    late, order = gate([late, order], [])
    extra_scores, loss, extra_part, extra = meet(
        [late, early, 0], None, extra_id * width + ids_in, loss, [jnp.bfloat16], [order], from_late
    )
    extra_part, order = gate([extra_part, order], [])
    order = pause(order, [extra_part])
    extra_part = permuted(extra_part, extra_back)

    rows_grad = rows_product(
        [own_scores, scores0, scores1, extra_scores],
        [student_head, mine0, theirs0, mine1, theirs1, extra],
        depth,
        [order],
    )
    head_grad = head_total(at, own_part, [back0, back1], extra_part)
    return (head_grad, rows_grad, loss[0])


def solution(mesh):
    placed = (
        P(("grp", "seq"), None),
        P(("grp", "seq"), None),
        P("seq", None),
        P("seq", None),
        P(("grp", "seq")),
        P(("grp", "seq")),
        P(("grp", "seq")),
    )
    return jax.shard_map(
        body,
        mesh=mesh,
        in_specs=placed,
        out_specs=(P(("grp", "seq"), None), P(("grp", "seq"), None), P(("grp", "seq"))),
        check_vma=False,
    )
```

```python
import jax
import jax.numpy as jnp
from jax import lax
from jax.experimental import pallas as pl
from jax.experimental.pallas import tpu as pltpu
from jax.sharding import PartitionSpec as P

hard_weight = 0.5
CHUNKS = 4
GATE_VMEM = 128 * 1024
MEETING_VMEM = 12 * 1024 * 1024
WIDE_VMEM = 56 * 1024 * 1024
BOTH = ("grp", "seq")


def permuted(value, move):
    groups, count = lax.axis_size("grp"), lax.axis_size("seq")
    pairs = []
    for group in range(groups):
        for place in range(count):
            target = move(group, place)
            if target is not None:
                pairs.append((group * count + place, target[0] * count + target[1] % count))
    return lax.ppermute(value, BOTH, pairs)


def next_chip(group, place):
    return group, place + 2


def previous_chip(group, place):
    return group, place - 2


def other_plane(group, place):
    return 1 - group, place


def other_core(group, place):
    return group, place + 1 - 2 * (place % 2)


def extra_early(group, place):
    if place % 2 == 0:
        return group, place + 1
    return (group, place + 3) if place // 2 % 2 == 0 else None


def extra_late(group, place):
    return (group, place + 3) if place % 2 == 1 and place // 2 % 2 == 1 else None


def extra_back(group, place):
    return group, place - 3 + 2 * (place % 2)


def gate(values, ready, flops=0):
    operands = list(values) + list(ready)
    anywhere = pl.BlockSpec(memory_space=pl.ANY)
    return pl.pallas_call(
        lambda *refs: None,
        out_shape=[jax.ShapeDtypeStruct(value.shape, value.dtype) for value in values],
        in_specs=[anywhere] * len(operands),
        out_specs=[anywhere] * len(values),
        input_output_aliases={index: index for index in range(len(values))},
        compiler_params=pltpu.CompilerParams(vmem_limit_bytes=GATE_VMEM),
        cost_estimate=pl.CostEstimate(flops=flops, bytes_accessed=0, transcendentals=0),
    )(*operands)


def packed(at, student_head, teacher_head, places, ready=()):
    depth, depth_t = student_head.shape[1], teacher_head.shape[1]

    def kernel(at_ref, student_ref, teacher_ref, *refs):
        outs, sems = refs[len(ready) : -1], refs[-1]
        copies = []
        for index, (moves, start, rows) in enumerate(places):
            first = pl.multiple_of(at_ref[0] + start, 16) if moves else start
            for half, (source, lo, wide) in enumerate(
                [(student_ref, 0, depth), (teacher_ref, depth, depth_t)]
            ):
                copies.append(
                    pltpu.make_async_copy(
                        source.at[pl.ds(first, rows), :],
                        outs[index].at[:, pl.ds(lo, wide)],
                        sems.at[2 * index + half],
                    )
                )
        for copy in copies:
            copy.start()
        for copy in copies:
            copy.wait()

    anywhere = pl.BlockSpec(memory_space=pl.ANY)
    return pl.pallas_call(
        kernel,
        out_shape=[
            jax.ShapeDtypeStruct((rows, depth + depth_t), student_head.dtype) for _, _, rows in places
        ],
        in_specs=[pl.BlockSpec(memory_space=pltpu.SMEM)]
        + [pl.BlockSpec(memory_space=pltpu.HBM)] * 2
        + [anywhere] * len(ready),
        out_specs=[anywhere] * len(places),
        scratch_shapes=[pltpu.SemaphoreType.DMA((2 * len(places),))],
        compiler_params=pltpu.CompilerParams(vmem_limit_bytes=GATE_VMEM),
    )(at, student_head, teacher_head, *ready)


def head_total(at, own_part, backs, extra):
    width, depth = own_part.shape
    half = width // 2
    quarter = half // 2
    whole = pl.BlockSpec(memory_space=pltpu.VMEM)

    def kernel(at_ref, own_ref, back0, back1, extra_ref, out_ref, sum_ref, sems):
        copies = []
        for stage, back in enumerate((back0, back1)):
            for side in range(2):
                base = at_ref[0] if side == 0 else half - at_ref[0]
                rows = pl.ds(pl.multiple_of(base + stage * quarter, quarter), quarter)
                sum_ref[rows, :] = (
                    own_ref[rows, :]
                    + back[pl.ds(side * quarter, quarter), :].astype(jnp.float32)
                    + extra_ref[rows, :].astype(jnp.float32)
                ).astype(sum_ref.dtype)
                copies.append(
                    pltpu.make_async_copy(
                        sum_ref.at[rows, :], out_ref.at[rows, :], sems.at[2 * stage + side]
                    )
                )
                copies[-1].start()
        for copy in copies:
            copy.wait()

    return pl.pallas_call(
        kernel,
        out_shape=jax.ShapeDtypeStruct((width, depth), jnp.bfloat16),
        in_specs=[pl.BlockSpec(memory_space=pltpu.SMEM)] + [whole] * 4,
        out_specs=pl.BlockSpec(memory_space=pl.ANY),
        scratch_shapes=[pltpu.VMEM((width, depth), jnp.bfloat16), pltpu.SemaphoreType.DMA((4,))],
        compiler_params=pltpu.CompilerParams(vmem_limit_bytes=6 * 1024 * 1024),
    )(at, own_part, *backs, extra)


def pause(order, ready):
    return gate([order], ready, 30_000_000_000)[0]


def free():
    return pl.CostEstimate(flops=0, bytes_accessed=0, transcendentals=0)


def meeting(rows_s, rows_t, panels, panels_t, norm, norm_t, targets, ids, loss, kinds, ready=(), flag=None):
    count, depth = rows_s.shape
    depth_t = rows_t.shape[1]
    start = 0
    if flag is not None:
        panels, start = panels[:2], panels[2]
        panels_t = []
    pieces = len(panels)
    pieces_t = len(panels_t)
    width = panels[0].shape[0] if flag is not None else sum(panel.shape[0] for panel in panels)
    block = count // 2
    part_rows = width // len(kinds)
    whole = pl.BlockSpec(memory_space=pltpu.VMEM)
    contract = (((1,), (1,)), ((), ()))
    flags = [] if flag is None else [flag]

    def kernel(*refs):
        s_ref, t_ref, norm_ref, norm_t_ref, target_ref, ids_ref, loss_in = refs[:7]
        panel_refs = refs[7 : 7 + pieces]
        panel_t_refs = refs[7 + pieces : 7 + pieces + pieces_t]
        flag_refs = refs[7 + pieces + pieces_t :][: len(flags)]
        outs = refs[7 + pieces + pieces_t + len(flags) + len(ready) :]
        score_ref, loss_ref = outs[:2]
        part_refs = outs[2 : 2 + len(kinds)]
        if flags:
            chosen = outs[-1]

            @pl.when(flag_refs[0][0] == 1)
            def _():
                chosen[...] = panel_refs[0][...]

            @pl.when(flag_refs[0][0] != 1)
            def _():
                chosen[...] = panel_refs[1][pl.ds(start, width), :]

            panel, panel_t = chosen[:, :depth], chosen[:, depth:]
        else:
            panel = jnp.concatenate([ref[:, :depth] for ref in panel_refs], axis=0)
            panel_t = jnp.concatenate(
                [ref[:, ref.shape[1] - depth_t :] for ref in panel_t_refs], axis=0
            )

        for step in range(2):
            rows = pl.ds(step * block, block)
            zs = lax.dot_general(s_ref[rows, :], panel, contract, preferred_element_type=jnp.float32)
            zt = lax.dot_general(t_ref[rows, :], panel_t, contract, preferred_element_type=jnp.float32)
            ls = zs - norm_ref[rows, :]
            lt = zt - norm_t_ref[rows, :]
            ps = jnp.exp(ls)
            pt = jnp.exp(lt)
            onehot = (target_ref[rows, :] == ids_ref[...]).astype(jnp.float32)
            scores = ((1.0 + hard_weight) * ps - pt - hard_weight * onehot).astype(jnp.bfloat16)
            score_ref[rows, :] = scores
            terms = pt * (lt - ls) - hard_weight * onehot * ls
            loss_ref[:, rows] = loss_in[:, rows] + lax.dot_general(
                jnp.ones((8, width), jnp.float32),
                terms,
                contract,
                precision=lax.Precision.HIGHEST,
                preferred_element_type=jnp.float32,
            )

        part = lax.dot_general(
            score_ref[...], s_ref[...], (((0,), (0,)), ((), ())), preferred_element_type=jnp.float32
        )
        for index, part_ref in enumerate(part_refs):
            part_ref[...] = part[index * part_rows : (index + 1) * part_rows].astype(part_ref.dtype)

    out_shape = [
        jax.ShapeDtypeStruct((count, width), jnp.bfloat16),
        jax.ShapeDtypeStruct((8, count), jnp.float32),
    ] + [jax.ShapeDtypeStruct((part_rows, depth), kind) for kind in kinds]
    if flags:
        out_shape.append(jax.ShapeDtypeStruct((width, depth + depth_t), jnp.bfloat16))
    return pl.pallas_call(
        kernel,
        out_shape=out_shape,
        in_specs=[whole] * (7 + pieces + pieces_t)
        + [pl.BlockSpec(memory_space=pltpu.SMEM)] * len(flags)
        + [pl.BlockSpec(memory_space=pl.ANY)] * len(ready),
        out_specs=[whole] * len(out_shape),
        compiler_params=pltpu.CompilerParams(vmem_limit_bytes=MEETING_VMEM),
        cost_estimate=free(),
    )(rows_s, rows_t, norm, norm_t, targets, ids, loss, *panels, *panels_t, *flags, *ready)


def rows_product(scores, panels, depth, ready):
    count = scores[0].shape[0]
    block = depth // 4
    inner = sum(panel.shape[0] for panel in panels)

    def kernel(*refs):
        score_refs = refs[: len(scores)]
        panel_refs = refs[len(scores) : len(scores) + len(panels)]
        out_ref, left_ref = refs[-2:]

        @pl.when(pl.program_id(0) == 0)
        def _():
            left_ref[...] = jnp.concatenate([ref[...] for ref in score_refs], axis=1)

        right = jnp.concatenate([ref[...] for ref in panel_refs], axis=0)
        out_ref[...] = jnp.dot(
            left_ref[...], right, preferred_element_type=jnp.float32
        ).astype(out_ref.dtype)

    return pl.pallas_call(
        kernel,
        grid=(4,),
        out_shape=jax.ShapeDtypeStruct((count, depth), jnp.bfloat16),
        in_specs=[pl.BlockSpec((count, score.shape[1]), lambda index: (0, 0)) for score in scores]
        + [pl.BlockSpec((panel.shape[0], block), lambda index: (0, index)) for panel in panels]
        + [pl.BlockSpec(memory_space=pl.ANY)] * len(ready),
        out_specs=pl.BlockSpec((count, block), lambda index: (0, index)),
        scratch_shapes=[pltpu.VMEM((count, inner), jnp.bfloat16)],
        compiler_params=pltpu.CompilerParams(vmem_limit_bytes=WIDE_VMEM),
        cost_estimate=pl.CostEstimate(flops=30_000_000_000, bytes_accessed=0, transcendentals=0),
    )(*scores, *panels, *ready)


def body(student_rows, teacher_rows, student_head, teacher_head, student_lse, teacher_lse, targets):
    count = lax.axis_size("seq")
    place = lax.axis_index("seq")
    plane = lax.axis_index("grp")
    core = place % 2
    width, depth = student_head.shape
    half = width // 2
    piece = half // CHUNKS
    norm = student_lse.astype(jnp.float32)[:, None]
    norm_t = teacher_lse.astype(jnp.float32)[:, None]
    wanted = targets[:, None]
    order = jnp.zeros((8, 128), jnp.float32)
    ids_in = jnp.arange(width, dtype=jnp.int32)
    near = (place - 2) % count
    far = (place - 1 - 2 * core) % count
    extra_id = jnp.where(core == 1, place - 1, place - 3) % count
    from_late = jnp.reshape(jnp.logical_and(core == 0, place // 2 % 2 == 1), (1,)).astype(jnp.int32)

    def stage_ids(stage):
        rows = jnp.arange(half // 2, dtype=jnp.int32) + stage * (half // 2)
        inside = jnp.concatenate([plane * half + rows, (1 - plane) * half + rows])
        return jnp.concatenate([near * width + inside, far * width + inside])

    def meet(panels, panels_t, ids, loss, kinds, ready, flag=None):
        return meeting(
            student_rows, teacher_rows, panels, panels_t, norm, norm_t, wanted, ids[None, :], loss, kinds, ready, flag
        )

    at = jnp.reshape(plane * half, (1,)).astype(jnp.int32)
    chunks = packed(at, student_head, teacher_head, [(True, k * piece, piece) for k in range(2)])
    chunks = list(chunks)
    chunks[0], = gate([chunks[0]], [])
    chunks[1], = gate([chunks[1]], [chunks[0]])
    chunks += packed(
        at,
        student_head,
        teacher_head,
        [(True, k * piece, piece) for k in range(2, 4)]
        + [(False, 0, width)] * 2,
    )
    send, send0 = chunks[4:]
    chunks = chunks[:4]

    crossed = [permuted(chunk, next_chip) for chunk in chunks]
    early = permuted(send, extra_early)
    swapped = [None] * 4
    order = pause(order, [chunks[0]])
    crossed[0], order = gate([crossed[0], order], [])
    swapped[0] = permuted(crossed[0], other_plane)
    order = pause(order, [crossed[0]])
    crossed[1], order = gate([crossed[1], order], [])
    swapped[1] = permuted(crossed[1], other_plane)
    order = pause(order, [crossed[1]])
    crossed[2], send0, order = gate([crossed[2], send0, order], [])
    swapped[2] = permuted(crossed[2], other_plane)
    late = permuted(send0, extra_late)
    own_scores, loss, own_part = meet(
        [student_head],
        [teacher_head],
        place * width + ids_in,
        jnp.zeros((8, student_rows.shape[0]), jnp.float32),
        [jnp.float32],
        [order],
    )
    order = pause(order, [crossed[2], send0, own_scores])
    swapped[0], swapped[1], order = gate([swapped[0], swapped[1], order], [])
    mine0 = jnp.concatenate([crossed[0], crossed[1], swapped[0], swapped[1]], axis=0)
    theirs0 = permuted(mine0, other_core)
    order = pause(order, [mine0])
    crossed[3], order = gate([crossed[3], order], [])
    swapped[3] = permuted(crossed[3], other_plane)

    order = pause(order, [])
    theirs0, early, order = gate([theirs0, early, order], [])
    pair = [mine0, theirs0]
    scores0, loss, keep, give = meet(pair, pair, stage_ids(0), loss, [jnp.float32, jnp.bfloat16], [order])
    got = permuted(give, other_core)
    order = pause(order, [give])
    got, order = gate([got, order], [])
    total = (keep + got.astype(jnp.float32)).astype(jnp.bfloat16)
    back0 = permuted(total, previous_chip)

    swapped[2], swapped[3], order = gate([swapped[2], swapped[3], order], [total])
    mine1 = jnp.concatenate([crossed[2], crossed[3], swapped[2], swapped[3]], axis=0)
    theirs1 = permuted(mine1, other_core)
    order = pause(order, [mine1])
    theirs1, order = gate([theirs1, order], [])
    pair = [mine1, theirs1]
    scores1, loss, keep, give = meet(pair, pair, stage_ids(1), loss, [jnp.float32, jnp.bfloat16], [order])
    got = permuted(give, other_core)
    order = pause(order, [give])
    got, order = gate([got, order], [])
    total = (keep + got.astype(jnp.float32)).astype(jnp.bfloat16)
    back1 = permuted(total, previous_chip)

    order = pause(order, [total])
    late, order = gate([late, order], [])
    extra_scores, loss, extra_part, extra = meet(
        [late, early, 0], None, extra_id * width + ids_in, loss, [jnp.bfloat16], [order], from_late
    )
    extra_part, order = gate([extra_part, order], [])
    order = pause(order, [extra_part])
    extra_part = permuted(extra_part, extra_back)

    rows_grad = rows_product(
        [own_scores, scores0, scores1, extra_scores],
        [student_head, mine0, theirs0, mine1, theirs1, extra],
        depth,
        [order],
    )
    head_grad = head_total(at, own_part, [back0, back1], extra_part)
    return (head_grad, rows_grad, loss[0])


def solution(mesh):
    placed = (
        P(("grp", "seq"), None),
        P(("grp", "seq"), None),
        P("seq", None),
        P("seq", None),
        P(("grp", "seq")),
        P(("grp", "seq")),
        P(("grp", "seq")),
    )
    return jax.shard_map(
        body,
        mesh=mesh,
        in_specs=placed,
        out_specs=(P(("grp", "seq"), None), P(("grp", "seq"), None), P(("grp", "seq"))),
        check_vma=False,
    )
```
